32 devices in a mesh: dp: 2 (over core), expert: 16 (over z, y, x).
Axes of the slice: x: 2, y: 2, z: 4, core: 2. Of those that a mesh axis runs over, the one named last changes fastest.
Arguments:
- tokens: bfloat16 [4096, 2048], P(('dp', 'expert')), may hold values from -6 to 6
- out_grad: bfloat16 [4096, 2048], P(('dp', 'expert')), may hold values from -6 to 6
- expert_ids: int32 [4096, 4], P(('dp', 'expert')), may hold values from 0 to 15, as said below
- gate_weights: float32 [4096, 4], P(('dp', 'expert')), may hold values from 0.05 to 0.6
- w_in: bfloat16 [16, 2048, 768], P('expert'), may hold values from -0.125 to 0.125
- w_out: bfloat16 [16, 384, 2048], P('expert'), may hold values from -0.3125 to 0.3125
Outputs:
- token_grad: bfloat16 [4096, 2048], P(('dp', 'expert'))
- w_in_grad: bfloat16 [16, 2048, 768], P('expert', 'dp')
- w_out_grad: bfloat16 [16, 384, 2048], P('expert', None, 'dp')
The draws below stay inside these ranges and needn't reach their ends.
Inputs may be any that keep to these rules, and one draw needn't show every extreme that they name: `expert_ids`: each token names 4 different experts; among the 128 tokens of one device no expert is named more than 56 times, and in every device's tokens some expert is named exactly 56 times.
All inputs are finite; a program needn't handle non-finite values.
Results may differ from the reference program's by a relative error of at most 0.0065.
Values may be sent and summed in bfloat16 or wider, within the bound.
A program may use at most 128 MiB of HBM per device.

```python
import math
import jax
import jax.numpy as jnp
from jax import lax

D = 2048
FF = 384
ROUTES = 4
TOK_DEV = 128
EXPERTS = 16
CAP = 56
TOKENS = 4096
DEVICES = 32


def draw_expert_ids(key, part):
    block_count = TOKENS // TOK_DEV
    order = jax.random.permutation(jax.random.fold_in(key, 11), EXPERTS).astype(jnp.int32)
    offset = jax.random.randint(jax.random.fold_in(key, 12), (block_count,), 0, EXPERTS - 1).astype(jnp.int32)
    block_index = jnp.arange(block_count, dtype=jnp.int32)
    chosen = order[block_index % EXPERTS]
    slot = jnp.arange(TOK_DEV * ROUTES, dtype=jnp.int32)
    marked_before = jnp.minimum((slot + ROUTES - 1) // ROUTES, CAP)
    marked = (slot % ROUTES == 0) & (slot // ROUTES < CAP)
    others = slot - marked_before
    rest = (chosen[:, None] + 1 + (offset[:, None] + others[None, :]) % (EXPERTS - 1)) % EXPERTS
    picked = jnp.where(marked[None, :], chosen[:, None], rest)
    return picked.reshape(TOKENS, ROUTES).astype(jnp.int32)


def levels(own_key, dims, split, smallest, high):
    factor_of, own = 1.0, jax.random.fold_in(own_key, 6)
    for position, shards_of in split:
        draws = jnp.exp(jax.random.uniform(jax.random.fold_in(own, position), (shards_of,), jnp.float32, smallest / len(split), high / len(split)))
        factor_of = factor_of * jnp.repeat(draws, dims[position] // shards_of).reshape([-1 if axis == position else 1 for axis in range(len(dims))])
    return factor_of


def noise(own_key, extent, deviation, reach, split=(), kind=jnp.bfloat16):
    result = deviation * jax.random.normal(own_key, extent, jnp.float32)
    if split:
        result = result * levels(own_key, extent, split, -0.22, 0.18)
    return jnp.clip(result, -reach, reach).astype(kind)


def setup_inputs(seed: int = 0) -> dict:
    splits = jax.random.split(jax.random.key(seed), 7)
    tokens = noise(splits[0], (TOKENS, D), 1.0, 6.0, ((0, 32),))
    out_grad = noise(splits[1], (TOKENS, D), 1.0, 6.0, ((0, 32),))
    expert_ids = draw_expert_ids(jax.random.fold_in(splits[6], 71), 0)
    gate_weights = jnp.clip(jnp.exp(math.log(0.6) - 2.4849067 * jax.random.uniform(splits[3], (TOKENS, ROUTES), jnp.float32) ** levels(splits[3], (TOKENS, ROUTES), ((0, 32),), -0.2, 0.2)), 0.05, 0.6)
    w_in = noise(splits[4], (EXPERTS, D, 2 * FF), D ** -0.5, 0.125, ((0, 16),))
    w_out = noise(splits[5], (EXPERTS, FF, D), FF ** -0.5, 0.3125, ((0, 16),))
    return {"tokens": tokens, "out_grad": out_grad, "expert_ids": expert_ids, "gate_weights": gate_weights, "w_in": w_in, "w_out": w_out}


def silu_parts(gate_part):
    sigma = 1.0 / (1.0 + jnp.exp(-gate_part))
    return gate_part * sigma, sigma * (1.0 + gate_part * (1.0 - sigma))


def expert_back(rows_in, rows_grad, weight_in, weight_out):
    hidden_width = weight_out.shape[0]
    joined = jnp.dot(rows_in, weight_in, preferred_element_type=jnp.float32)
    gate_part = joined[:, :hidden_width]
    up_part = joined[:, hidden_width:]
    activated, derivative = silu_parts(gate_part)
    hidden = (activated * up_part).astype(jnp.bfloat16)
    d_hidden = lax.dot_general(rows_grad, weight_out, (((1,), (1,)), ((), ())), preferred_element_type=jnp.float32)
    d_joined = jnp.concatenate([d_hidden * up_part * derivative, d_hidden * activated], axis=1).astype(jnp.bfloat16)
    d_rows = lax.dot_general(d_joined, weight_in, (((1,), (1,)), ((), ())), preferred_element_type=jnp.float32).astype(jnp.bfloat16)
    grad_in = lax.dot_general(rows_in, d_joined, (((0,), (0,)), ((), ())), preferred_element_type=jnp.float32)
    grad_out = lax.dot_general(hidden, rows_grad, (((0,), (0,)), ((), ())), preferred_element_type=jnp.float32)
    return d_rows, grad_in, grad_out


def reference(tokens, out_grad, expert_ids, gate_weights, w_in, w_out):
    flat_ids = expert_ids.reshape(-1).astype(jnp.int32)
    total_routes = flat_ids.shape[0]
    route_tok = (jnp.arange(total_routes, dtype=jnp.int32) // ROUTES).astype(jnp.int32)
    gate_flat = gate_weights.reshape(-1)
    sorted_routes = jnp.argsort(flat_ids, stable=True).astype(jnp.int32)
    counts = jnp.bincount(flat_ids, length=EXPERTS).astype(jnp.int32)
    offsets = (jnp.cumsum(counts) - counts).astype(jnp.int32)
    most_rows = DEVICES * CAP
    padded = jnp.concatenate([sorted_routes, jnp.zeros((most_rows,), jnp.int32)])

    def per_expert(carry, expert):
        route_index = lax.dynamic_slice(padded, (offsets[expert].astype(jnp.int32),), (most_rows,))
        live_rows = jnp.arange(most_rows, dtype=jnp.int32) < counts[expert]
        token_rows = route_tok[route_index]
        rows_in = tokens[token_rows]
        scaled = gate_flat[route_index][:, None] * out_grad[token_rows].astype(jnp.float32)
        rows_grad = jnp.where(live_rows[:, None], scaled, jnp.zeros((), jnp.float32)).astype(jnp.bfloat16)
        d_rows, grad_in, grad_out = expert_back(rows_in, rows_grad, w_in[expert], w_out[expert])
        carry = carry.at[token_rows].add(d_rows.astype(jnp.float32))
        return carry, (grad_in.astype(jnp.bfloat16), grad_out.astype(jnp.bfloat16))

    start = jnp.zeros(tokens.shape, jnp.float32)
    summed, grads = lax.scan(per_expert, start, jnp.arange(EXPERTS, dtype=jnp.int32))
    return summed.astype(jnp.bfloat16), grads[0], grads[1]
```

```python
import jax
import jax.numpy as jnp
from jax import lax
from jax.sharding import PartitionSpec as P


def silu_parts(gate_part):
    sigma = 1.0 / (1.0 + jnp.exp(-gate_part))
    return (gate_part * sigma, sigma * (1.0 + gate_part * (1.0 - sigma)))


def backward_rows(rows_in, rows_grad, weight_in, weight_out):
    hidden_width = weight_out.shape[0]
    joined = jnp.dot(rows_in, weight_in, preferred_element_type=jnp.float32)
    gate_part = joined[:, :hidden_width]
    up_part = joined[:, hidden_width:]
    activated, derivative = silu_parts(gate_part)
    hidden = (activated * up_part).astype(jnp.bfloat16)
    d_hidden = lax.dot_general(
        rows_grad, weight_out, (((1,), (1,)), ((), ())), preferred_element_type=jnp.float32
    )
    d_joined = jnp.concatenate(
        [d_hidden * up_part * derivative, d_hidden * activated], axis=1
    ).astype(jnp.bfloat16)
    d_rows = lax.dot_general(
        d_joined, weight_in, (((1,), (1,)), ((), ())), preferred_element_type=jnp.float32
    ).astype(jnp.bfloat16)
    grad_in = lax.dot_general(
        rows_in, d_joined, (((0,), (0,)), ((), ())), preferred_element_type=jnp.float32
    )
    grad_out = lax.dot_general(
        hidden, rows_grad, (((0,), (0,)), ((), ())), preferred_element_type=jnp.float32
    )
    return (d_rows, grad_in, grad_out)


def selection(ids, weights, experts, capacity):
    count = ids.shape[0]
    hit = ids[:, :, None] == experts[None, None, :]
    member = jnp.any(hit, axis=1)
    weight = jnp.sum(jnp.where(hit, weights[:, :, None], 0.0), axis=1)
    earlier = (
        jnp.arange(count, dtype=jnp.int32)[:, None] > jnp.arange(count, dtype=jnp.int32)[None, :]
    ).astype(jnp.bfloat16)
    rank = jnp.dot(earlier, member.astype(jnp.bfloat16), preferred_element_type=jnp.float32)
    rank = jnp.where(member, rank.astype(jnp.int32), -1)
    chosen = rank.T[:, None, :] == jnp.arange(capacity, dtype=jnp.int32)[None, :, None]
    slot_weight = jnp.sum(jnp.where(chosen, weight.T[:, None, :], 0.0), axis=2)
    return chosen.astype(jnp.bfloat16), slot_weight


def body(tokens, out_grad, expert_ids, gate_weights, w_in, w_out):
    hosts = lax.axis_size("expert")
    token_count, model_width = tokens.shape
    capacity = 7 * token_count * expert_ids.shape[1] // (4 * hosts)
    pick, slot_weight = selection(
        expert_ids, gate_weights, jnp.arange(hosts, dtype=jnp.int32), capacity
    )
    pick = pick.reshape(hosts * capacity, token_count)
    send_in = jnp.dot(pick, tokens, preferred_element_type=jnp.float32).astype(jnp.bfloat16)
    send_grad = (
        slot_weight.reshape(-1, 1) * jnp.dot(pick, out_grad, preferred_element_type=jnp.float32)
    ).astype(jnp.bfloat16)
    got_in = lax.all_to_all(send_in, "expert", split_axis=0, concat_axis=0, tiled=True)
    got_grad = lax.all_to_all(send_grad, "expert", split_axis=0, concat_axis=0, tiled=True)
    d_rows, grad_in, grad_out = backward_rows(got_in, got_grad, w_in[0], w_out[0])
    returned = lax.all_to_all(d_rows, "expert", split_axis=0, concat_axis=0, tiled=True)
    sum_in = lax.psum_scatter(grad_in, "dp", scatter_dimension=0, tiled=True)
    sum_out = lax.psum_scatter(grad_out, "dp", scatter_dimension=1, tiled=True)
    token_grad = lax.dot_general(
        pick, returned, (((0,), (0,)), ((), ())), preferred_element_type=jnp.float32
    ).astype(jnp.bfloat16)
    return (token_grad, sum_in.astype(jnp.bfloat16)[None], sum_out.astype(jnp.bfloat16)[None])


def solution(mesh):
    in_specs = (
        P(("dp", "expert"), None),
        P(("dp", "expert"), None),
        P(("dp", "expert"), None),
        P(("dp", "expert"), None),
        P("expert", None, None),
        P("expert", None, None),
    )
    out_specs = (P(("dp", "expert"), None), P("expert", "dp", None), P("expert", None, "dp"))
    return jax.shard_map(body, mesh=mesh, in_specs=in_specs, out_specs=out_specs, check_vma=False)
```

```python
import functools
import jax
import jax.numpy as jnp
from jax import lax
from jax.experimental import pallas as pl
from jax.experimental.pallas import tpu as pltpu
from jax.sharding import PartitionSpec as P


def silu_parts(gate_part):
    sigma = 1.0 / (1.0 + jnp.exp(-gate_part))
    return (gate_part * sigma, sigma * (1.0 + gate_part * (1.0 - sigma)))


def backward_rows(rows_in, rows_grad, weight_in, weight_out):
    hidden_width = weight_out.shape[0]
    joined = jnp.dot(rows_in, weight_in, preferred_element_type=jnp.float32)
    gate_part = joined[:, :hidden_width]
    up_part = joined[:, hidden_width:]
    activated, derivative = silu_parts(gate_part)
    hidden = (activated * up_part).astype(jnp.bfloat16)
    d_hidden = lax.dot_general(
        rows_grad, weight_out, (((1,), (1,)), ((), ())), preferred_element_type=jnp.float32
    )
    d_joined = jnp.concatenate(
        [d_hidden * up_part * derivative, d_hidden * activated], axis=1
    ).astype(jnp.bfloat16)
    d_rows = lax.dot_general(
        d_joined, weight_in, (((1,), (1,)), ((), ())), preferred_element_type=jnp.float32
    ).astype(jnp.bfloat16)
    grad_in = lax.dot_general(
        rows_in, d_joined, (((0,), (0,)), ((), ())), preferred_element_type=jnp.float32
    )
    grad_out = lax.dot_general(
        hidden, rows_grad, (((0,), (0,)), ((), ())), preferred_element_type=jnp.float32
    )
    return (d_rows, grad_in, grad_out)


def selection(ids, weights, experts, capacity):
    count = ids.shape[0]
    hit = ids[:, :, None] == experts[None, None, :]
    member = jnp.any(hit, axis=1)
    weight = jnp.sum(jnp.where(hit, weights[:, :, None], 0.0), axis=1)
    earlier = (
        jnp.arange(count, dtype=jnp.int32)[:, None] > jnp.arange(count, dtype=jnp.int32)[None, :]
    ).astype(jnp.bfloat16)
    rank = jnp.dot(earlier, member.astype(jnp.bfloat16), preferred_element_type=jnp.float32)
    rank = jnp.where(member, rank.astype(jnp.int32), -1)
    chosen = rank.T[:, None, :] == jnp.arange(capacity, dtype=jnp.int32)[None, :, None]
    slot_weight = jnp.sum(jnp.where(chosen, weight.T[:, None, :], 0.0), axis=2)
    return chosen.astype(jnp.bfloat16), slot_weight


PLANES = 4
INNER = 4
MESH = pl.DeviceIdType.MESH


def flipped(p, d):
    x, y = p % 2, p // 2
    if d % 2:
        x = 1 - x
    if d // 2:
        y = 1 - y
    return 2 * y + x


def fused_kernel(
    capacity,
    tok_ref,
    og_ref,
    meta_ref,
    w_in_ref,
    w_out_ref,
    tg_ref,
    gin_ref,
    gout_ref,
    ztok,
    zog,
    zmeta,
    send_in,
    send_gr,
    got_in,
    got_gr,
    d_rows,
    ret,
    hid,
    dj,
    part,
    part_got,
    peer_in,
    peer_out,
    far_in,
    far_out,
    z_send,
    z_recv,
    meta_send,
    meta_recv,
    p_send,
    p_recv,
    r_send,
    r_recv,
    t_send,
    t_recv,
    g_send,
    g_recv,
):
    me = lax.axis_index("expert")
    core = lax.axis_index("dp")
    z, p = me // INNER, me % INNER
    count, width = tok_ref.shape
    ff = w_out_ref.shape[0]
    rows = 2 * capacity
    block_rows = INNER * rows
    wide = 512
    odd = z % 2
    pair = z // 2
    partner = z + 1 - 2 * odd
    is_inner = jnp.logical_or(z == 1, z == 2)
    near = 2 - pair
    far = 3 * (1 - pair)
    zdev = lambda s: {"expert": s * INNER + p}
    pdev = lambda d: {"expert": z * INNER + flipped(p, d)}

    def remote(src, dst, send_sem, recv_sem, device):
        return pltpu.make_async_remote_copy(
            src_ref=src,
            dst_ref=dst,
            send_sem=send_sem,
            recv_sem=recv_sem,
            device_id=device,
            device_id_type=MESH,
        )

    barrier = pltpu.get_barrier_semaphore()
    for k in range(1, PLANES):
        pl.semaphore_signal(barrier, inc=1, device_id=zdev((z + k) % PLANES), device_id_type=MESH)
    for d in range(1, INNER):
        pl.semaphore_signal(barrier, inc=1, device_id=pdev(d), device_id_type=MESH)
    pl.semaphore_signal(barrier, inc=1, device_id={"dp": 1 - core}, device_id_type=MESH)
    pl.semaphore_wait(barrier, PLANES + INNER - 1)

    held = (ztok, zog)
    own = (tok_ref, og_ref)

    def meta_copy(s):
        return remote(meta_ref, zmeta.at[z], meta_send.at[s], meta_recv.at[z], zdev(s))

    def arrive_meta(s):
        remote(meta_ref, zmeta.at[s], meta_send.at[s], meta_recv.at[s], zdev(s)).wait_recv()

    def own_copy(a, k, to):
        return remote(own[a], held[a].at[z], z_send.at[a, k], z_recv.at[a, z], zdev(to))

    def pass_on(a, k, s, to):
        return remote(held[a].at[s], held[a].at[s], z_send.at[a, k], z_recv.at[a, s], zdev(to))

    def arrive(a, s):
        remote(held[a].at[s], held[a].at[s], z_send.at[a, 0], z_recv.at[a, s], zdev(s)).wait_recv()

    others = [(z + k) % PLANES for k in range(1, PLANES)]
    cross = near
    for s in others:
        meta_copy(s).start()
    for a in range(2):
        own_copy(a, 0, partner).start()

        @pl.when(is_inner)
        def _():
            own_copy(a, 1, cross).start()

    ztok[z] = tok_ref[...]
    zog[z] = og_ref[...]
    zmeta[z] = meta_ref[...]

    row_id = lax.broadcasted_iota(jnp.int32, (rows, count), 0).astype(jnp.float32)

    def planes_of(b):
        first = 2 * pair if b == 0 else 2 * (1 - pair)
        return (first, first + 1)

    def chosen(s, half, d):
        expert = z * INNER + flipped(p, d)
        code = zmeta[s, pl.ds(expert, 1), :]
        return row_id == code + float(half * capacity)

    def plane_copy(a, b, d):
        src = (send_in, send_gr)[a]
        dst = (got_in, got_gr)[a]
        at = pl.ds(b * block_rows + d * rows, rows)
        return remote(src.at[at], dst.at[at], p_send.at[a, b, d], p_recv.at[a, b, d], pdev(d))

    def dispatch(a, b):
        lo, hi = planes_of(b)
        for d in (3, 1, 2, 0):
            pick_lo, pick_hi = chosen(lo, 0, d), chosen(hi, 1, d)
            sel_lo, sel_hi = pick_lo.astype(jnp.bfloat16), pick_hi.astype(jnp.bfloat16)
            if a == 1:
                expert = z * INNER + flipped(p, d)
                scale = jnp.sum(
                    jnp.where(pick_lo, zmeta[lo, pl.ds(expert + PLANES * INNER, 1), :], 0.0)
                    + jnp.where(pick_hi, zmeta[hi, pl.ds(expert + PLANES * INNER, 1), :], 0.0),
                    axis=1,
                    keepdims=True,
                )
            out = ((got_in, got_gr) if d == 0 else (send_in, send_gr))[a]
            at = pl.ds(b * block_rows + d * rows, rows)

            @pl.loop(0, width // wide)
            def _(c):
                cols = pl.ds(pl.multiple_of(c * wide, wide), wide)
                picked = jnp.dot(
                    sel_lo, held[a][lo, :, cols], preferred_element_type=jnp.float32
                ) + jnp.dot(sel_hi, held[a][hi, :, cols], preferred_element_type=jnp.float32)
                if a == 1:
                    picked = picked * scale
                out[at, cols] = picked.astype(jnp.bfloat16)

            if d:
                plane_copy(a, b, d).start()

    arrive(0, partner)

    @pl.when(is_inner)
    def _():
        pass_on(0, 2, partner, cross).start()

    arrive_meta(partner)
    dispatch(0, 0)
    arrive(1, partner)

    @pl.when(is_inner)
    def _():
        pass_on(1, 2, partner, cross).start()
        for a in range(2):
            arrive(a, near)
            pass_on(a, 3, near, partner).start()

    dispatch(1, 0)

    @pl.when(is_inner)
    def _():
        for a in range(2):
            arrive(a, far)
            pass_on(a, 4, far, partner).start()

    arrive_meta(near)
    arrive_meta(far)
    for a in range(2):

        @pl.when(jnp.logical_not(is_inner))
        def _():
            arrive(a, near)
            arrive(a, far)

        dispatch(a, 1)

    def back_rows(b):
        for a in range(2):
            for d in range(1, INNER):
                plane_copy(a, b, d).wait_recv()
        tile = block_rows // 2

        @pl.loop(0, 2)
        def _(t):
            at = pl.ds(pl.multiple_of(b * block_rows + t * tile, 16), tile)
            joined = jnp.dot(got_in[at, :], w_in_ref[...], preferred_element_type=jnp.float32)
            gate_part, up_part = joined[:, :ff], joined[:, ff:]
            activated, derivative = silu_parts(gate_part)
            hid[at, :] = (activated * up_part).astype(jnp.bfloat16)
            d_hidden = lax.dot_general(
                got_gr[at, :],
                w_out_ref[...],
                (((1,), (1,)), ((), ())),
                preferred_element_type=jnp.float32,
            )
            dj[at, :ff] = (d_hidden * up_part * derivative).astype(jnp.bfloat16)
            dj[at, ff:] = (d_hidden * activated).astype(jnp.bfloat16)

            @pl.loop(0, width // wide)
            def _(c):
                cols = pl.ds(pl.multiple_of(c * wide, wide), wide)
                d_rows[at, cols] = lax.dot_general(
                    dj[at, :],
                    w_in_ref[cols, :],
                    (((1,), (1,)), ((), ())),
                    preferred_element_type=jnp.float32,
                ).astype(jnp.bfloat16)

    def back_copy(b, d):
        at = pl.ds(b * block_rows + d * rows, rows)
        return remote(d_rows.at[at], ret.at[at], r_send.at[b, d], r_recv.at[b, d], pdev(d))

    def part_copy(s):
        return remote(part.at[s], part_got.at[z], t_send.at[s], t_recv.at[z], zdev(s))

    def combine(b, half):
        s = planes_of(b)[half]
        sels = [chosen(s, half, d).astype(jnp.bfloat16) for d in range(INNER)]

        @pl.loop(0, width // wide)
        def _(c):
            cols = pl.ds(pl.multiple_of(c * wide, wide), wide)
            total = jnp.zeros((count, wide), jnp.float32)
            for d in range(INNER):
                at = pl.ds(b * block_rows + d * rows, rows)
                total = total + lax.dot_general(
                    sels[d],
                    (ret if d else d_rows)[at, cols],
                    (((0,), (0,)), ((), ())),
                    preferred_element_type=jnp.float32,
                )
            part[s, :, cols] = total.astype(jnp.bfloat16)

    back_rows(0)
    back_rows(1)
    for b in (1, 0):
        for d in (3, 1, 2):
            back_copy(b, d).start()

    half_width = width // 2
    tile = 256

    def weight_tiles(cols):
        to_in = lax.dot_general(
            got_in[:, cols], dj[...], (((0,), (0,)), ((), ())), preferred_element_type=jnp.float32
        )
        to_out = lax.dot_general(
            hid[...], got_gr[:, cols], (((0,), (0,)), ((), ())), preferred_element_type=jnp.float32
        )
        return to_in, to_out

    @pl.loop(0, half_width // tile)
    def _(c):
        at = pl.ds(pl.multiple_of(c * tile, tile), tile)
        cols = pl.ds(pl.multiple_of((1 - core) * half_width + c * tile, tile), tile)
        to_in, to_out = weight_tiles(cols)
        peer_in[at, :] = to_in
        peer_out[:, at] = to_out

    swaps = [
        remote(peer_in, far_in, g_send.at[0], g_recv.at[0], {"dp": 1 - core}),
        remote(peer_out, far_out, g_send.at[1], g_recv.at[1], {"dp": 1 - core}),
    ]
    for copy in swaps:
        copy.start()

    for d in range(1, INNER):
        back_copy(1, d).wait_recv()
    for half, s in enumerate(planes_of(1)):
        combine(1, half)
        part_copy(s).start()

    for copy in swaps:
        copy.wait_recv()

    @pl.loop(0, half_width // tile)
    def _(c):
        at = pl.ds(pl.multiple_of(c * tile, tile), tile)
        cols = pl.ds(pl.multiple_of(core * half_width + c * tile, tile), tile)
        to_in, to_out = weight_tiles(cols)
        gin_ref[at, :] = (to_in + far_in[at, :]).astype(jnp.bfloat16)
        gout_ref[:, at] = (to_out + far_out[:, at]).astype(jnp.bfloat16)

    for d in range(1, INNER):
        back_copy(0, d).wait_recv()
    for half in range(2):
        combine(0, half)
    part_copy(partner).start()

    for s in others:
        remote(part.at[s], part_got.at[s], t_send.at[s], t_recv.at[s], zdev(s)).wait_recv()

    @pl.loop(0, width // wide)
    def _(c):
        cols = pl.ds(pl.multiple_of(c * wide, wide), wide)
        total = part[z, :, cols].astype(jnp.float32)
        for s in others:
            total = total + part_got[s, :, cols].astype(jnp.float32)
        tg_ref[:, cols] = total.astype(jnp.bfloat16)

    for s in others:
        meta_copy(s).wait_send()
        part_copy(s).wait_send()
    for a in range(2):
        own_copy(a, 0, partner).wait_send()

        @pl.when(is_inner)
        def _():
            own_copy(a, 1, cross).wait_send()
            pass_on(a, 2, partner, cross).wait_send()
            pass_on(a, 3, near, partner).wait_send()
            pass_on(a, 4, far, partner).wait_send()

    for b in range(2):
        for d in range(1, INNER):
            for a in range(2):
                plane_copy(a, b, d).wait_send()
            back_copy(b, d).wait_send()
    for copy in swaps:
        copy.wait_send()


def fused(capacity, tokens, out_grad, expert_ids, gate_weights, w_in, w_out):
    hosts = PLANES * INNER
    count, width = tokens.shape
    ff = w_out.shape[1]
    hit = expert_ids.T[:, None, :] == jnp.arange(hosts, dtype=jnp.int32)[None, :, None]
    member = jnp.any(hit, axis=0)
    weight = jnp.sum(jnp.where(hit, gate_weights.T[:, None, :], 0.0), axis=0)
    order = jnp.arange(count, dtype=jnp.int32)
    earlier = (order[:, None] < order[None, :]).astype(jnp.bfloat16)
    rank = jnp.dot(member.astype(jnp.bfloat16), earlier, preferred_element_type=jnp.float32)
    code = jnp.where(member, rank, -1024.0)
    meta = jnp.concatenate([code, weight], axis=0)
    slots = 2 * INNER * 2 * capacity
    vmem = pl.BlockSpec(memory_space=pltpu.VMEM)
    bf16, f32, dma = jnp.bfloat16, jnp.float32, pltpu.SemaphoreType.DMA
    token_grad, grad_in, grad_out = pl.pallas_call(
        functools.partial(fused_kernel, capacity),
        out_shape=[
            jax.ShapeDtypeStruct((count, width), bf16),
            jax.ShapeDtypeStruct((width // 2, 2 * ff), bf16),
            jax.ShapeDtypeStruct((ff, width // 2), bf16),
        ],
        in_specs=[vmem] * 5,
        out_specs=[vmem] * 3,
        scratch_shapes=[
            pltpu.VMEM((PLANES, count, width), bf16),
            pltpu.VMEM((PLANES, count, width), bf16),
            pltpu.VMEM((PLANES, 2 * hosts, count), f32),
            pltpu.VMEM((slots, width), bf16),
            pltpu.VMEM((slots, width), bf16),
            pltpu.VMEM((slots, width), bf16),
            pltpu.VMEM((slots, width), bf16),
            pltpu.VMEM((slots, width), bf16),
            pltpu.VMEM((slots, width), bf16),
            pltpu.VMEM((slots, ff), bf16),
            pltpu.VMEM((slots, 2 * ff), bf16),
            pltpu.VMEM((PLANES, count, width), bf16),
            pltpu.VMEM((PLANES, count, width), bf16),
            pltpu.VMEM((width // 2, 2 * ff), f32),
            pltpu.VMEM((ff, width // 2), f32),
            pltpu.VMEM((width // 2, 2 * ff), f32),
            pltpu.VMEM((ff, width // 2), f32),
            dma((2, 5)),
            dma((2, PLANES)),
            dma((PLANES,)),
            dma((PLANES,)),
            dma((2, 2, INNER)),
            dma((2, 2, INNER)),
            dma((2, INNER)),
            dma((2, INNER)),
            dma((PLANES,)),
            dma((PLANES,)),
            dma((2,)),
            dma((2,)),
        ],
        compiler_params=pltpu.CompilerParams(
            collective_id=0, has_side_effects=True, vmem_limit_bytes=60 * 2**20
        ),
        cost_estimate=pl.CostEstimate(
            flops=2 * slots * width * ff * 8, bytes_accessed=12 * 2**20, transcendentals=slots * ff
        ),
    )(tokens, out_grad, meta, w_in[0], w_out[0])
    return token_grad, grad_in[None], grad_out[None]


def body(tokens, out_grad, expert_ids, gate_weights, w_in, w_out):
    hosts = lax.axis_size("expert")
    token_count, model_width = tokens.shape
    capacity = 7 * token_count * expert_ids.shape[1] // (4 * hosts)
    if hosts == 16 and 2 * capacity % 16 == 0:
        return fused(capacity, tokens, out_grad, expert_ids, gate_weights, w_in, w_out)
    pick, slot_weight = selection(
        expert_ids, gate_weights, jnp.arange(hosts, dtype=jnp.int32), capacity
    )
    pick = pick.reshape(hosts * capacity, token_count)
    send_in = jnp.dot(pick, tokens, preferred_element_type=jnp.float32).astype(jnp.bfloat16)
    send_grad = (
        slot_weight.reshape(-1, 1) * jnp.dot(pick, out_grad, preferred_element_type=jnp.float32)
    ).astype(jnp.bfloat16)
    got_in = lax.all_to_all(send_in, "expert", split_axis=0, concat_axis=0, tiled=True)
    got_grad = lax.all_to_all(send_grad, "expert", split_axis=0, concat_axis=0, tiled=True)
    d_rows, grad_in, grad_out = backward_rows(got_in, got_grad, w_in[0], w_out[0])
    returned = lax.all_to_all(d_rows, "expert", split_axis=0, concat_axis=0, tiled=True)
    sum_in = lax.psum_scatter(grad_in, "dp", scatter_dimension=0, tiled=True)
    sum_out = lax.psum_scatter(grad_out, "dp", scatter_dimension=1, tiled=True)
    token_grad = lax.dot_general(
        pick, returned, (((0,), (0,)), ((), ())), preferred_element_type=jnp.float32
    ).astype(jnp.bfloat16)
    return (token_grad, sum_in.astype(jnp.bfloat16)[None], sum_out.astype(jnp.bfloat16)[None])


def solution(mesh):
    in_specs = (
        P(("dp", "expert"), None),
        P(("dp", "expert"), None),
        P(("dp", "expert"), None),
        P(("dp", "expert"), None),
        P("expert", None, None),
        P("expert", None, None),
    )
    out_specs = (P(("dp", "expert"), None), P("expert", "dp", None), P("expert", None, "dp"))
    return jax.shard_map(body, mesh=mesh, in_specs=in_specs, out_specs=out_specs, check_vma=False)
```

```python
import functools
import jax
import jax.numpy as jnp
from jax import lax
from jax.experimental import pallas as pl
from jax.experimental.pallas import tpu as pltpu
from jax.sharding import PartitionSpec as P


def silu_parts(gate_part):
    sigma = 1.0 / (1.0 + jnp.exp(-gate_part))
    return (gate_part * sigma, sigma * (1.0 + gate_part * (1.0 - sigma)))


def backward_rows(rows_in, rows_grad, weight_in, weight_out):
    hidden_width = weight_out.shape[0]
    joined = jnp.dot(rows_in, weight_in, preferred_element_type=jnp.float32)
    gate_part = joined[:, :hidden_width]
    up_part = joined[:, hidden_width:]
    activated, derivative = silu_parts(gate_part)
    hidden = (activated * up_part).astype(jnp.bfloat16)
    d_hidden = lax.dot_general(
        rows_grad, weight_out, (((1,), (1,)), ((), ())), preferred_element_type=jnp.float32
    )
    d_joined = jnp.concatenate(
        [d_hidden * up_part * derivative, d_hidden * activated], axis=1
    ).astype(jnp.bfloat16)
    d_rows = lax.dot_general(
        d_joined, weight_in, (((1,), (1,)), ((), ())), preferred_element_type=jnp.float32
    ).astype(jnp.bfloat16)
    grad_in = lax.dot_general(
        rows_in, d_joined, (((0,), (0,)), ((), ())), preferred_element_type=jnp.float32
    )
    grad_out = lax.dot_general(
        hidden, rows_grad, (((0,), (0,)), ((), ())), preferred_element_type=jnp.float32
    )
    return (d_rows, grad_in, grad_out)


def selection(ids, weights, experts, capacity):
    count = ids.shape[0]
    hit = ids[:, :, None] == experts[None, None, :]
    member = jnp.any(hit, axis=1)
    weight = jnp.sum(jnp.where(hit, weights[:, :, None], 0.0), axis=1)
    earlier = (
        jnp.arange(count, dtype=jnp.int32)[:, None] > jnp.arange(count, dtype=jnp.int32)[None, :]
    ).astype(jnp.bfloat16)
    rank = jnp.dot(earlier, member.astype(jnp.bfloat16), preferred_element_type=jnp.float32)
    rank = jnp.where(member, rank.astype(jnp.int32), -1)
    chosen = rank.T[:, None, :] == jnp.arange(capacity, dtype=jnp.int32)[None, :, None]
    slot_weight = jnp.sum(jnp.where(chosen, weight.T[:, None, :], 0.0), axis=2)
    return chosen.astype(jnp.bfloat16), slot_weight


PLANES = 4
INNER = 4
MESH = pl.DeviceIdType.MESH


def flipped(p, d):
    x, y = p % 2, p // 2
    if d % 2:
        x = 1 - x
    if d // 2:
        y = 1 - y
    return 2 * y + x


def fused_kernel(
    capacity,
    tok_ref,
    og_ref,
    meta_ref,
    w_in_hbm,
    w_out_hbm,
    tg_ref,
    gin_hbm,
    gout_hbm,
    w_in_ref,
    w_out_ref,
    gin_ref,
    gout_ref,
    joined_ref,
    ztok,
    zog,
    zmeta,
    send_in,
    send_gr,
    got_in,
    got_gr,
    d_rows,
    ret,
    hid,
    dj,
    part,
    part_got,
    peer_in,
    peer_out,
    far_in,
    far_out,
    z_send,
    z_recv,
    meta_send,
    meta_recv,
    p_send,
    p_recv,
    r_send,
    r_recv,
    t_send,
    t_recv,
    g_send,
    g_recv,
    local_sem,
):
    me = lax.axis_index("expert")
    core = lax.axis_index("dp")
    z, p = me // INNER, me % INNER
    count, width = tok_ref.shape
    ff = w_out_ref.shape[0]
    rows = 2 * capacity
    block_rows = INNER * rows
    wide = 512
    odd = z % 2
    pair = z // 2
    partner = z + 1 - 2 * odd
    is_inner = jnp.logical_or(z == 1, z == 2)
    near = 2 - pair
    far = 3 * (1 - pair)
    zdev = lambda s: {"expert": s * INNER + p}
    pdev = lambda d: {"expert": z * INNER + flipped(p, d)}

    def remote(src, dst, send_sem, recv_sem, device):
        return pltpu.make_async_remote_copy(
            src_ref=src,
            dst_ref=dst,
            send_sem=send_sem,
            recv_sem=recv_sem,
            device_id=device,
            device_id_type=MESH,
        )

    loads = [
        pltpu.make_async_copy(w_in_hbm, w_in_ref, local_sem.at[0]),
        pltpu.make_async_copy(w_out_hbm, w_out_ref, local_sem.at[1]),
    ]
    stores = [
        pltpu.make_async_copy(gin_ref, gin_hbm, local_sem.at[2]),
        pltpu.make_async_copy(gout_ref, gout_hbm, local_sem.at[3]),
    ]
    barrier = pltpu.get_barrier_semaphore()
    for k in range(1, PLANES):
        pl.semaphore_signal(barrier, inc=1, device_id=zdev((z + k) % PLANES), device_id_type=MESH)
    for d in range(1, INNER):
        pl.semaphore_signal(barrier, inc=1, device_id=pdev(d), device_id_type=MESH)
    pl.semaphore_signal(barrier, inc=1, device_id={"dp": 1 - core}, device_id_type=MESH)
    pl.semaphore_wait(barrier, PLANES + INNER - 1)

    held = (ztok, zog)
    own = (tok_ref, og_ref)

    def meta_copy(s):
        return remote(meta_ref, zmeta.at[z], meta_send.at[s], meta_recv.at[z], zdev(s))

    def arrive_meta(s):
        remote(meta_ref, zmeta.at[s], meta_send.at[s], meta_recv.at[s], zdev(s)).wait_recv()

    def own_copy(a, k, to):
        return remote(own[a], held[a].at[z], z_send.at[a, k], z_recv.at[a, z], zdev(to))

    def pass_on(a, k, s, to):
        return remote(held[a].at[s], held[a].at[s], z_send.at[a, k], z_recv.at[a, s], zdev(to))

    def arrive(a, s):
        remote(held[a].at[s], held[a].at[s], z_send.at[a, 0], z_recv.at[a, s], zdev(s)).wait_recv()

    others = [(z + k) % PLANES for k in range(1, PLANES)]
    cross = near
    for s in others:
        meta_copy(s).start()
    for a in range(2):
        own_copy(a, 0, partner).start()

        @pl.when(is_inner)
        def _():
            own_copy(a, 1, cross).start()

    for copy in loads:
        copy.start()
    ztok[z] = tok_ref[...]
    zog[z] = og_ref[...]
    zmeta[z] = meta_ref[...]

    row_id = lax.broadcasted_iota(jnp.int32, (rows, count), 0).astype(jnp.float32)

    def planes_of(b):
        return (z, partner) if b == 0 else (near, far)

    def chosen(s, half, d):
        expert = z * INNER + flipped(p, d)
        code = zmeta[s, pl.ds(expert, 1), :]
        return row_id == code + float(half * capacity)

    ready = capacity // 16 * 16
    pieces = ((0, 0, ready), (0, ready, rows - ready), (1, 0, rows))

    def plane_copy(a, piece, d):
        b, start, size = pieces[piece]
        src = (send_in, send_gr)[a]
        dst = (got_in, got_gr)[a]
        at = pl.ds(b * block_rows + d * rows + start, size)
        return remote(
            src.at[at], dst.at[at], p_send.at[a, piece, d], p_recv.at[a, piece, d], pdev(d)
        )

    def dispatch(a, piece):
        b, start, size = pieces[piece]
        planes = planes_of(b)[: 1 if piece == 0 else 2]
        for d in (3, 1, 2, 0):
            picks = [chosen(s, half, d)[start : start + size] for half, s in enumerate(planes)]
            sels = [pick.astype(jnp.bfloat16) for pick in picks]
            if a == 1:
                expert = z * INNER + flipped(p, d) + PLANES * INNER
                scale = jnp.sum(
                    sum(
                        jnp.where(pick, zmeta[s, pl.ds(expert, 1), :], 0.0)
                        for pick, s in zip(picks, planes)
                    ),
                    axis=1,
                    keepdims=True,
                )
            out = ((got_in, got_gr) if d == 0 else (send_in, send_gr))[a]
            at = pl.ds(b * block_rows + d * rows + start, size)

            @pl.loop(0, width // wide)
            def _(c):
                cols = pl.ds(pl.multiple_of(c * wide, wide), wide)
                picked = sum(
                    jnp.dot(sel, held[a][s, :, cols], preferred_element_type=jnp.float32)
                    for sel, s in zip(sels, planes)
                )
                if a == 1:
                    picked = picked * scale
                out[at, cols] = picked.astype(jnp.bfloat16)

            if d:
                plane_copy(a, piece, d).start()

    dispatch(0, 0)
    dispatch(1, 0)

    arrive(0, partner)

    @pl.when(is_inner)
    def _():
        pass_on(0, 2, partner, cross).start()

    arrive_meta(partner)
    dispatch(0, 1)
    arrive(1, partner)

    @pl.when(is_inner)
    def _():
        pass_on(1, 2, partner, cross).start()
        for a in range(2):
            arrive(a, near)
            pass_on(a, 3, near, partner).start()

    dispatch(1, 1)

    @pl.when(is_inner)
    def _():
        for a in range(2):
            arrive(a, far)
            pass_on(a, 4, far, partner).start()

    arrive_meta(near)
    arrive_meta(far)
    for a in range(2):

        @pl.when(jnp.logical_not(is_inner))
        def _():
            arrive(a, near)
            arrive(a, far)

        dispatch(a, 2)

    def arrive_rows(a, b):
        for d in range(1, INNER):
            for piece in range(len(pieces)):
                if pieces[piece][0] == b:
                    plane_copy(a, piece, d).wait_recv()

    tile_rows = block_rows // 2
    quarters = width // wide

    def joined_rows(b):
        @pl.loop(0, 2)
        def _(t):
            at = pl.ds(pl.multiple_of(b * block_rows + t * tile_rows, 16), tile_rows)
            joined_ref[pl.ds(pl.multiple_of(t * tile_rows, 16), tile_rows), :] = jnp.dot(
                got_in[at, :], w_in_ref[...], preferred_element_type=jnp.float32
            )

    def hidden_rows(b):
        @pl.loop(0, 2)
        def _(t):
            at = pl.ds(pl.multiple_of(b * block_rows + t * tile_rows, 16), tile_rows)
            here = pl.ds(pl.multiple_of(t * tile_rows, 16), tile_rows)
            gate_part, up_part = joined_ref[here, :ff], joined_ref[here, ff:]
            activated, derivative = silu_parts(gate_part)
            hid[at, :] = (activated * up_part).astype(jnp.bfloat16)
            d_hidden = lax.dot_general(
                got_gr[at, :],
                w_out_ref[...],
                (((1,), (1,)), ((), ())),
                preferred_element_type=jnp.float32,
            )
            dj[at, :ff] = (d_hidden * up_part * derivative).astype(jnp.bfloat16)
            dj[at, ff:] = (d_hidden * activated).astype(jnp.bfloat16)

    def input_rows(b, c):
        at = pl.ds(b * block_rows, block_rows)
        cols = pl.ds(c * wide, wide)
        d_rows[at, cols] = lax.dot_general(
            dj[at, :],
            w_in_ref[cols, :],
            (((1,), (1,)), ((), ())),
            preferred_element_type=jnp.float32,
        ).astype(jnp.bfloat16)

    def back_copy(b, d, c):
        at = (pl.ds(b * block_rows + d * rows, rows), pl.ds(c * wide, wide))
        return remote(d_rows.at[at], ret.at[at], r_send.at[b, d, c], r_recv.at[b, d, c], pdev(d))

    def part_copy(s, c):
        cols = pl.ds(c * wide, wide)
        return remote(
            part.at[s, :, cols],
            part_got.at[z, :, cols],
            t_send.at[s, c],
            t_recv.at[z, c],
            zdev(s),
        )

    def combine(b, half, c):
        s = planes_of(b)[half]
        cols = pl.ds(c * wide, wide)
        total = jnp.zeros((count, wide), jnp.float32)
        for d in range(INNER):
            at = pl.ds(b * block_rows + d * rows, rows)
            total = total + lax.dot_general(
                chosen(s, half, d).astype(jnp.bfloat16),
                (ret if d else d_rows)[at, cols],
                (((0,), (0,)), ((), ())),
                preferred_element_type=jnp.float32,
            )
        part[s, :, cols] = total.astype(jnp.bfloat16)

    for copy in loads:
        copy.wait()
    arrive_rows(0, 0)
    joined_rows(0)
    arrive_rows(1, 0)
    hidden_rows(0)
    for c in range(quarters):
        input_rows(0, c)
    arrive_rows(0, 1)
    joined_rows(1)
    arrive_rows(1, 1)
    early = [(3, c) for c in range(quarters // 2)]
    late = [(d, c) for c in range(quarters) for d in (3, 1, 2) if (d, c) not in early]
    for d, c in early:
        back_copy(0, d, c).start()
    hidden_rows(1)
    for c in range(quarters):
        input_rows(1, c)
        for d in (3, 1, 2):
            back_copy(1, d, c).start()
    for d, c in late:
        back_copy(0, d, c).start()

    half_width = width // 2
    tile = 256

    def weight_tiles(cols):
        to_in = lax.dot_general(
            got_in[:, cols], dj[...], (((0,), (0,)), ((), ())), preferred_element_type=jnp.float32
        )
        to_out = lax.dot_general(
            hid[...], got_gr[:, cols], (((0,), (0,)), ((), ())), preferred_element_type=jnp.float32
        )
        return to_in, to_out

    @pl.loop(0, half_width // tile)
    def _(c):
        at = pl.ds(pl.multiple_of(c * tile, tile), tile)
        cols = pl.ds(pl.multiple_of((1 - core) * half_width + c * tile, tile), tile)
        to_in, to_out = weight_tiles(cols)
        peer_in[at, :] = to_in
        peer_out[:, at] = to_out

    swaps = [
        remote(peer_in, far_in, g_send.at[0], g_recv.at[0], {"dp": 1 - core}),
        remote(peer_out, far_out, g_send.at[1], g_recv.at[1], {"dp": 1 - core}),
    ]
    for copy in swaps:
        copy.start()

    for c in range(quarters):
        for d in range(1, INNER):
            back_copy(1, d, c).wait_recv()
        for half, s in ((1, far), (0, near)):
            combine(1, half, c)
            part_copy(s, c).start()

    for copy in swaps:
        copy.wait_recv()

    @pl.loop(0, half_width // tile)
    def _(c):
        at = pl.ds(pl.multiple_of(c * tile, tile), tile)
        cols = pl.ds(pl.multiple_of(core * half_width + c * tile, tile), tile)
        to_in, to_out = weight_tiles(cols)
        gin_ref[at, :] = (to_in + far_in[at, :]).astype(jnp.bfloat16)
        gout_ref[:, at] = (to_out + far_out[:, at]).astype(jnp.bfloat16)

    for copy in stores:
        copy.start()

    for c in range(quarters):
        for d in range(1, INNER):
            back_copy(0, d, c).wait_recv()
        combine(0, 1, c)
        part_copy(partner, c).start()
        combine(0, 0, c)

    for c in range(quarters):
        cols = pl.ds(c * wide, wide)
        total = part[z, :, cols].astype(jnp.float32)
        for s in others:
            remote(
                part.at[s, :, cols],
                part_got.at[s, :, cols],
                t_send.at[s, c],
                t_recv.at[s, c],
                zdev(s),
            ).wait_recv()
            total = total + part_got[s, :, cols].astype(jnp.float32)
        tg_ref[:, cols] = total.astype(jnp.bfloat16)

    for s in others:
        meta_copy(s).wait_send()
        for c in range(quarters):
            part_copy(s, c).wait_send()
    for a in range(2):
        own_copy(a, 0, partner).wait_send()

        @pl.when(is_inner)
        def _():
            own_copy(a, 1, cross).wait_send()
            pass_on(a, 2, partner, cross).wait_send()
            pass_on(a, 3, near, partner).wait_send()
            pass_on(a, 4, far, partner).wait_send()

    for d in range(1, INNER):
        for a in range(2):
            for piece in range(len(pieces)):
                plane_copy(a, piece, d).wait_send()
        for b in range(2):
            for c in range(quarters):
                back_copy(b, d, c).wait_send()
    for copy in swaps:
        copy.wait_send()
    for copy in stores:
        copy.wait()


def fused(capacity, tokens, out_grad, expert_ids, gate_weights, w_in, w_out):
    hosts = PLANES * INNER
    count, width = tokens.shape
    ff = w_out.shape[1]
    hit = expert_ids.T[:, None, :] == jnp.arange(hosts, dtype=jnp.int32)[None, :, None]
    member = jnp.any(hit, axis=0)
    weight = jnp.sum(jnp.where(hit, gate_weights.T[:, None, :], 0.0), axis=0)
    order = jnp.arange(count, dtype=jnp.int32)
    earlier = (order[:, None] < order[None, :]).astype(jnp.bfloat16)
    rank = jnp.dot(member.astype(jnp.bfloat16), earlier, preferred_element_type=jnp.float32)
    code = jnp.where(member, rank, -1024.0)
    meta = jnp.concatenate([code, weight], axis=0)
    slots = 2 * INNER * 2 * capacity
    vmem = pl.BlockSpec(memory_space=pltpu.VMEM)
    hbm = pl.BlockSpec(memory_space=pl.ANY)
    quarters = width // 512
    bf16, f32, dma = jnp.bfloat16, jnp.float32, pltpu.SemaphoreType.DMA
    token_grad, grad_in, grad_out = pl.pallas_call(
        functools.partial(fused_kernel, capacity),
        out_shape=[
            jax.ShapeDtypeStruct((count, width), bf16),
            jax.ShapeDtypeStruct((width // 2, 2 * ff), bf16),
            jax.ShapeDtypeStruct((ff, width // 2), bf16),
        ],
        in_specs=[vmem] * 3 + [hbm] * 2,
        out_specs=[vmem, hbm, hbm],
        scratch_shapes=[
            pltpu.VMEM((width, 2 * ff), bf16),
            pltpu.VMEM((ff, width), bf16),
            pltpu.VMEM((width // 2, 2 * ff), bf16),
            pltpu.VMEM((ff, width // 2), bf16),
            pltpu.VMEM((slots // 2, 2 * ff), f32),
            pltpu.VMEM((PLANES, count, width), bf16),
            pltpu.VMEM((PLANES, count, width), bf16),
            pltpu.VMEM((PLANES, 2 * hosts, count), f32),
            pltpu.VMEM((slots, width), bf16),
            pltpu.VMEM((slots, width), bf16),
            pltpu.VMEM((slots, width), bf16),
            pltpu.VMEM((slots, width), bf16),
            pltpu.VMEM((slots, width), bf16),
            pltpu.VMEM((slots, width), bf16),
            pltpu.VMEM((slots, ff), bf16),
            pltpu.VMEM((slots, 2 * ff), bf16),
            pltpu.VMEM((PLANES, count, width), bf16),
            pltpu.VMEM((PLANES, count, width), bf16),
            pltpu.VMEM((width // 2, 2 * ff), f32),
            pltpu.VMEM((ff, width // 2), f32),
            pltpu.VMEM((width // 2, 2 * ff), f32),
            pltpu.VMEM((ff, width // 2), f32),
            dma((2, 5)),
            dma((2, PLANES)),
            dma((PLANES,)),
            dma((PLANES,)),
            dma((2, 3, INNER)),
            dma((2, 3, INNER)),
            dma((2, INNER, quarters)),
            dma((2, INNER, quarters)),
            dma((PLANES, quarters)),
            dma((PLANES, quarters)),
            dma((2,)),
            dma((2,)),
            dma((4,)),
        ],
        compiler_params=pltpu.CompilerParams(
            collective_id=0, has_side_effects=True, vmem_limit_bytes=60 * 2**20
        ),
        cost_estimate=pl.CostEstimate(
            flops=2 * slots * width * ff * 8, bytes_accessed=12 * 2**20, transcendentals=slots * ff
        ),
    )(tokens, out_grad, meta, w_in[0], w_out[0])
    return token_grad, grad_in[None], grad_out[None]


def body(tokens, out_grad, expert_ids, gate_weights, w_in, w_out):
    hosts = lax.axis_size("expert")
    token_count, model_width = tokens.shape
    capacity = 7 * token_count * expert_ids.shape[1] // (4 * hosts)
    if hosts == 16 and 2 * capacity % 16 == 0:
        return fused(capacity, tokens, out_grad, expert_ids, gate_weights, w_in, w_out)
    pick, slot_weight = selection(
        expert_ids, gate_weights, jnp.arange(hosts, dtype=jnp.int32), capacity
    )
    pick = pick.reshape(hosts * capacity, token_count)
    send_in = jnp.dot(pick, tokens, preferred_element_type=jnp.float32).astype(jnp.bfloat16)
    send_grad = (
        slot_weight.reshape(-1, 1) * jnp.dot(pick, out_grad, preferred_element_type=jnp.float32)
    ).astype(jnp.bfloat16)
    got_in = lax.all_to_all(send_in, "expert", split_axis=0, concat_axis=0, tiled=True)
    got_grad = lax.all_to_all(send_grad, "expert", split_axis=0, concat_axis=0, tiled=True)
    d_rows, grad_in, grad_out = backward_rows(got_in, got_grad, w_in[0], w_out[0])
    returned = lax.all_to_all(d_rows, "expert", split_axis=0, concat_axis=0, tiled=True)
    sum_in = lax.psum_scatter(grad_in, "dp", scatter_dimension=0, tiled=True)
    sum_out = lax.psum_scatter(grad_out, "dp", scatter_dimension=1, tiled=True)
    token_grad = lax.dot_general(
        pick, returned, (((0,), (0,)), ((), ())), preferred_element_type=jnp.float32
    ).astype(jnp.bfloat16)
    return (token_grad, sum_in.astype(jnp.bfloat16)[None], sum_out.astype(jnp.bfloat16)[None])


def solution(mesh):
    in_specs = (
        P(("dp", "expert"), None),
        P(("dp", "expert"), None),
        P(("dp", "expert"), None),
        P(("dp", "expert"), None),
        P("expert", None, None),
        P("expert", None, None),
    )
    out_specs = (P(("dp", "expert"), None), P("expert", "dp", None), P("expert", None, "dp"))
    return jax.shard_map(body, mesh=mesh, in_specs=in_specs, out_specs=out_specs, check_vma=False)
```

```python
import functools
import jax
import jax.numpy as jnp
from jax import lax
from jax.experimental import pallas as pl
from jax.experimental.pallas import tpu as pltpu
from jax.sharding import PartitionSpec as P


def silu_parts(gate_part):
    sigma = 1.0 / (1.0 + jnp.exp(-gate_part))
    return (gate_part * sigma, sigma * (1.0 + gate_part * (1.0 - sigma)))


def backward_rows(rows_in, rows_grad, weight_in, weight_out):
    hidden_width = weight_out.shape[0]
    joined = jnp.dot(rows_in, weight_in, preferred_element_type=jnp.float32)
    gate_part = joined[:, :hidden_width]
    up_part = joined[:, hidden_width:]
    activated, derivative = silu_parts(gate_part)
    hidden = (activated * up_part).astype(jnp.bfloat16)
    d_hidden = lax.dot_general(
        rows_grad, weight_out, (((1,), (1,)), ((), ())), preferred_element_type=jnp.float32
    )
    d_joined = jnp.concatenate(
        [d_hidden * up_part * derivative, d_hidden * activated], axis=1
    ).astype(jnp.bfloat16)
    d_rows = lax.dot_general(
        d_joined, weight_in, (((1,), (1,)), ((), ())), preferred_element_type=jnp.float32
    ).astype(jnp.bfloat16)
    grad_in = lax.dot_general(
        rows_in, d_joined, (((0,), (0,)), ((), ())), preferred_element_type=jnp.float32
    )
    grad_out = lax.dot_general(
        hidden, rows_grad, (((0,), (0,)), ((), ())), preferred_element_type=jnp.float32
    )
    return (d_rows, grad_in, grad_out)


def selection(ids, weights, experts, capacity):
    count = ids.shape[0]
    hit = ids[:, :, None] == experts[None, None, :]
    member = jnp.any(hit, axis=1)
    weight = jnp.sum(jnp.where(hit, weights[:, :, None], 0.0), axis=1)
    earlier = (
        jnp.arange(count, dtype=jnp.int32)[:, None] > jnp.arange(count, dtype=jnp.int32)[None, :]
    ).astype(jnp.bfloat16)
    rank = jnp.dot(earlier, member.astype(jnp.bfloat16), preferred_element_type=jnp.float32)
    rank = jnp.where(member, rank.astype(jnp.int32), -1)
    chosen = rank.T[:, None, :] == jnp.arange(capacity, dtype=jnp.int32)[None, :, None]
    slot_weight = jnp.sum(jnp.where(chosen, weight.T[:, None, :], 0.0), axis=2)
    return chosen.astype(jnp.bfloat16), slot_weight


PLANES = 4
INNER = 4
MESH = pl.DeviceIdType.MESH


def flipped(p, d):
    x, y = p % 2, p // 2
    if d % 2:
        x = 1 - x
    if d // 2:
        y = 1 - y
    return 2 * y + x


def fused_kernel(
    capacity,
    tok_ref,
    og_ref,
    meta_ref,
    w_in_hbm,
    w_out_hbm,
    tg_ref,
    gin_hbm,
    gout_hbm,
    w_in_ref,
    w_out_ref,
    gin_ref,
    gout_ref,
    joined_ref,
    ztok,
    zog,
    zmeta,
    send_in,
    send_gr,
    got_in,
    got_gr,
    d_rows,
    ret,
    hid,
    dj,
    part,
    part_got,
    kept,
    peer_in,
    peer_out,
    far_in,
    far_out,
    z_send,
    z_recv,
    meta_send,
    meta_recv,
    p_send,
    p_recv,
    r_send,
    r_recv,
    t_send,
    t_recv,
    g_send,
    g_recv,
    local_sem,
):
    me = lax.axis_index("expert")
    core = lax.axis_index("dp")
    z, p = me // INNER, me % INNER
    count, width = tok_ref.shape
    ff = w_out_ref.shape[0]
    rows = 2 * capacity
    block_rows = INNER * rows
    wide = 512
    odd = z % 2
    pair = z // 2
    partner = z + 1 - 2 * odd
    is_inner = jnp.logical_or(z == 1, z == 2)
    near = 2 - pair
    far = 3 * (1 - pair)
    zdev = lambda s: {"expert": s * INNER + p}
    pdev = lambda d: {"expert": z * INNER + flipped(p, d)}

    def remote(src, dst, send_sem, recv_sem, device):
        return pltpu.make_async_remote_copy(
            src_ref=src,
            dst_ref=dst,
            send_sem=send_sem,
            recv_sem=recv_sem,
            device_id=device,
            device_id_type=MESH,
        )

    loads = [
        pltpu.make_async_copy(w_in_hbm, w_in_ref, local_sem.at[0]),
        pltpu.make_async_copy(w_out_hbm, w_out_ref, local_sem.at[1]),
    ]
    stores = [
        pltpu.make_async_copy(gin_ref, gin_hbm, local_sem.at[2]),
        pltpu.make_async_copy(gout_ref, gout_hbm, local_sem.at[3]),
    ]
    barrier = pltpu.get_barrier_semaphore()
    for k in range(1, PLANES):
        pl.semaphore_signal(barrier, inc=1, device_id=zdev((z + k) % PLANES), device_id_type=MESH)
    for d in range(1, INNER):
        pl.semaphore_signal(barrier, inc=1, device_id=pdev(d), device_id_type=MESH)
    pl.semaphore_signal(barrier, inc=1, device_id={"dp": 1 - core}, device_id_type=MESH)
    pl.semaphore_wait(barrier, PLANES + INNER - 1)

    held = (ztok, zog)
    own = (tok_ref, og_ref)

    def meta_copy(s):
        return remote(meta_ref, zmeta.at[z], meta_send.at[s], meta_recv.at[z], zdev(s))

    def arrive_meta(s):
        remote(meta_ref, zmeta.at[s], meta_send.at[s], meta_recv.at[s], zdev(s)).wait_recv()

    def own_copy(a, k, to):
        return remote(own[a], held[a].at[z], z_send.at[a, k], z_recv.at[a, z], zdev(to))

    def pass_on(a, k, s, to):
        return remote(held[a].at[s], held[a].at[s], z_send.at[a, k], z_recv.at[a, s], zdev(to))

    def arrive(a, s):
        remote(held[a].at[s], held[a].at[s], z_send.at[a, 0], z_recv.at[a, s], zdev(s)).wait_recv()

    others = [(z + k) % PLANES for k in range(1, PLANES)]
    cross = near
    for s in others:
        meta_copy(s).start()
    for a in range(2):
        own_copy(a, 0, partner).start()

        @pl.when(is_inner)
        def _():
            own_copy(a, 1, cross).start()

    for copy in loads:
        copy.start()
    ztok[z] = tok_ref[...]
    zog[z] = og_ref[...]
    zmeta[z] = meta_ref[...]

    row_id = lax.broadcasted_iota(jnp.int32, (rows, count), 0).astype(jnp.float32)

    def planes_of(b):
        return (z, partner) if b == 0 else (near, far)

    def chosen(s, half, d):
        expert = z * INNER + flipped(p, d)
        code = zmeta[s, pl.ds(expert, 1), :]
        return row_id == code + float(half * capacity)

    ready = capacity // 16 * 16
    pieces = tuple((b, *cut) for b in range(2) for cut in ((0, ready), (ready, rows - ready)))

    def plane_copy(a, piece, d):
        b, start, size = pieces[piece]
        src = (send_in, send_gr)[a]
        dst = (got_in, got_gr)[a]
        at = pl.ds(b * block_rows + d * rows + start, size)
        return remote(
            src.at[at], dst.at[at], p_send.at[a, piece, d], p_recv.at[a, piece, d], pdev(d)
        )

    def dispatch(a, piece):
        b, start, size = pieces[piece]
        planes = planes_of(b)[: 1 if start == 0 else 2]
        for d in (3, 1, 2, 0):
            picks = [chosen(s, half, d)[start : start + size] for half, s in enumerate(planes)]
            sels = [pick.astype(jnp.bfloat16) for pick in picks]
            if a == 1:
                expert = z * INNER + flipped(p, d) + PLANES * INNER
                scale = jnp.sum(
                    sum(
                        jnp.where(pick, zmeta[s, pl.ds(expert, 1), :], 0.0)
                        for pick, s in zip(picks, planes)
                    ),
                    axis=1,
                    keepdims=True,
                )
            out = ((got_in, got_gr) if d == 0 else (send_in, send_gr))[a]
            at = pl.ds(b * block_rows + d * rows + start, size)

            @pl.loop(0, width // wide)
            def _(c):
                cols = pl.ds(pl.multiple_of(c * wide, wide), wide)
                picked = sum(
                    jnp.dot(sel, held[a][s, :, cols], preferred_element_type=jnp.float32)
                    for sel, s in zip(sels, planes)
                )
                if a == 1:
                    picked = picked * scale
                out[at, cols] = picked.astype(jnp.bfloat16)

            if d:
                plane_copy(a, piece, d).start()

    dispatch(0, 0)
    dispatch(1, 0)

    arrive(0, partner)

    @pl.when(is_inner)
    def _():
        pass_on(0, 2, partner, cross).start()

    arrive_meta(partner)
    dispatch(0, 1)
    arrive(1, partner)

    @pl.when(is_inner)
    def _():
        pass_on(1, 2, partner, cross).start()
        for a in range(2):
            arrive(a, near)
            pass_on(a, 3, near, partner).start()

    dispatch(1, 1)

    arrive_meta(near)
    arrive_meta(far)
    for a in range(2):

        @pl.when(jnp.logical_not(is_inner))
        def _():
            arrive(a, near)

        dispatch(a, 2)

        if a == 0:

            @pl.when(is_inner)
            def _():
                for other in range(2):
                    arrive(other, far)
                    pass_on(other, 4, far, partner).start()

    for a in range(2):

        @pl.when(jnp.logical_not(is_inner))
        def _():
            arrive(a, far)

        dispatch(a, 3)

    def arrive_rows(a, b):
        for d in range(1, INNER):
            for piece in range(len(pieces)):
                if pieces[piece][0] == b:
                    plane_copy(a, piece, d).wait_recv()

    tile_rows = block_rows // 2
    quarters = width // wide

    def joined_rows(b):
        @pl.loop(0, 2)
        def _(t):
            at = pl.ds(pl.multiple_of(b * block_rows + t * tile_rows, 16), tile_rows)
            joined_ref[pl.ds(pl.multiple_of(t * tile_rows, 16), tile_rows), :] = jnp.dot(
                got_in[at, :], w_in_ref[...], preferred_element_type=jnp.float32
            )

    def hidden_rows(b):
        @pl.loop(0, 2)
        def _(t):
            at = pl.ds(pl.multiple_of(b * block_rows + t * tile_rows, 16), tile_rows)
            here = pl.ds(pl.multiple_of(t * tile_rows, 16), tile_rows)
            gate_part, up_part = joined_ref[here, :ff], joined_ref[here, ff:]
            activated, derivative = silu_parts(gate_part)
            hid[at, :] = (activated * up_part).astype(jnp.bfloat16)
            d_hidden = lax.dot_general(
                got_gr[at, :],
                w_out_ref[...],
                (((1,), (1,)), ((), ())),
                preferred_element_type=jnp.float32,
            )
            dj[at, :ff] = (d_hidden * up_part * derivative).astype(jnp.bfloat16)
            dj[at, ff:] = (d_hidden * activated).astype(jnp.bfloat16)

    def input_rows(b, c):
        at = pl.ds(b * block_rows, block_rows)
        cols = pl.ds(c * wide, wide)
        d_rows[at, cols] = lax.dot_general(
            dj[at, :],
            w_in_ref[cols, :],
            (((1,), (1,)), ((), ())),
            preferred_element_type=jnp.float32,
        ).astype(jnp.bfloat16)

    def back_copy(b, d, c):
        at = (pl.ds(b * block_rows + d * rows, rows), pl.ds(c * wide, wide))
        return remote(d_rows.at[at], ret.at[at], r_send.at[b, d, c], r_recv.at[b, d, c], pdev(d))

    from_end_near, from_end_far, from_partner, from_cross, from_cross_far = range(5)

    def part_copy(slot, land, to, c):
        cols = pl.ds(c * wide, wide)
        return remote(
            part.at[slot, :, cols],
            part_got.at[land, :, cols],
            t_send.at[slot, c],
            t_recv.at[land, c],
            zdev(to),
        )

    def landed(land, c):
        cols = pl.ds(c * wide, wide)
        part_copy(0, land, partner, c).wait_recv()
        return part_got[land, :, cols].astype(jnp.float32)

    def send_part(total, slot, land, to, c):
        part[slot, :, pl.ds(c * wide, wide)] = total.astype(jnp.bfloat16)
        part_copy(slot, land, to, c).start()

    def combine(b, half, c):
        s = planes_of(b)[half]
        cols = pl.ds(c * wide, wide)
        total = jnp.zeros((count, wide), jnp.float32)
        for d in range(INNER):
            at = pl.ds(b * block_rows + d * rows, rows)
            total = total + lax.dot_general(
                chosen(s, half, d).astype(jnp.bfloat16),
                (ret if d else d_rows)[at, cols],
                (((0,), (0,)), ((), ())),
                preferred_element_type=jnp.float32,
            )
        return total

    for copy in loads:
        copy.wait()
    arrive_rows(0, 0)
    joined_rows(0)
    arrive_rows(1, 0)
    hidden_rows(0)
    for c in range(quarters):
        input_rows(0, c)
    arrive_rows(0, 1)
    joined_rows(1)
    arrive_rows(1, 1)
    early = [(3, c) for c in range(quarters // 2)]
    late = [(d, c) for c in range(quarters) for d in (3, 1, 2) if (d, c) not in early]
    for d, c in early:
        back_copy(0, d, c).start()
    hidden_rows(1)
    for c in range(quarters):
        input_rows(1, c)
        for d in (3, 1, 2):
            back_copy(1, d, c).start()
    for d, c in late:
        back_copy(0, d, c).start()

    half_width = width // 2
    tile = 256

    def weight_tiles(cols):
        to_in = lax.dot_general(
            got_in[:, cols], dj[...], (((0,), (0,)), ((), ())), preferred_element_type=jnp.float32
        )
        to_out = lax.dot_general(
            hid[...], got_gr[:, cols], (((0,), (0,)), ((), ())), preferred_element_type=jnp.float32
        )
        return to_in, to_out

    @pl.loop(0, half_width // tile)
    def _(c):
        at = pl.ds(pl.multiple_of(c * tile, tile), tile)
        cols = pl.ds(pl.multiple_of((1 - core) * half_width + c * tile, tile), tile)
        to_in, to_out = weight_tiles(cols)
        peer_in[at, :] = to_in
        peer_out[:, at] = to_out

    swaps = [
        remote(peer_in, far_in, g_send.at[0], g_recv.at[0], {"dp": 1 - core}),
        remote(peer_out, far_out, g_send.at[1], g_recv.at[1], {"dp": 1 - core}),
    ]
    for copy in swaps:
        copy.start()

    for c in range(quarters):
        for d in range(1, INNER):
            back_copy(1, d, c).wait_recv()
        totals = [combine(1, half, c) for half in range(2)]

        @pl.when(is_inner)
        def _():
            for k in range(2):
                send_part(totals[k] + landed(from_end_near + k, c), k, from_cross + k, near, c)

        @pl.when(jnp.logical_not(is_inner))
        def _():
            for k in range(2):
                send_part(totals[k], k, from_end_near + k, partner, c)

    for copy in swaps:
        copy.wait_recv()

    @pl.loop(0, half_width // tile)
    def _(c):
        at = pl.ds(pl.multiple_of(c * tile, tile), tile)
        cols = pl.ds(pl.multiple_of(core * half_width + c * tile, tile), tile)
        to_in, to_out = weight_tiles(cols)
        gin_ref[at, :] = (to_in + far_in[at, :]).astype(jnp.bfloat16)
        gout_ref[:, at] = (to_out + far_out[:, at]).astype(jnp.bfloat16)

    for copy in stores:
        copy.start()

    for c in range(quarters):
        for d in range(1, INNER):
            back_copy(0, d, c).wait_recv()
        total = combine(0, 1, c)

        @pl.when(is_inner)
        def _():
            send_part(total + landed(from_cross_far, c), 2, from_partner, partner, c)

        @pl.when(jnp.logical_not(is_inner))
        def _():
            send_part(total, 2, from_partner, partner, c)

        kept[:, pl.ds(c * wide, wide)] = combine(0, 0, c)

    for c in range(quarters):
        cols = pl.ds(c * wide, wide)
        kept[:, cols] += landed(from_partner, c)

        @pl.when(is_inner)
        def _():
            kept[:, cols] += landed(from_cross, c)

        tg_ref[:, cols] = kept[:, cols].astype(jnp.bfloat16)

    for s in others:
        meta_copy(s).wait_send()
    for slot in range(3):
        for c in range(quarters):
            part_copy(slot, from_partner, partner, c).wait_send()
    for a in range(2):
        own_copy(a, 0, partner).wait_send()

        @pl.when(is_inner)
        def _():
            own_copy(a, 1, cross).wait_send()
            pass_on(a, 2, partner, cross).wait_send()
            pass_on(a, 3, near, partner).wait_send()
            pass_on(a, 4, far, partner).wait_send()

    for d in range(1, INNER):
        for a in range(2):
            for piece in range(len(pieces)):
                plane_copy(a, piece, d).wait_send()
        for b in range(2):
            for c in range(quarters):
                back_copy(b, d, c).wait_send()
    for copy in swaps:
        copy.wait_send()
    for copy in stores:
        copy.wait()


def fused(capacity, tokens, out_grad, expert_ids, gate_weights, w_in, w_out):
    hosts = PLANES * INNER
    count, width = tokens.shape
    ff = w_out.shape[1]
    hit = expert_ids.T[:, None, :] == jnp.arange(hosts, dtype=jnp.int32)[None, :, None]
    member = jnp.any(hit, axis=0)
    weight = jnp.sum(jnp.where(hit, gate_weights.T[:, None, :], 0.0), axis=0)
    order = jnp.arange(count, dtype=jnp.int32)
    earlier = (order[:, None] < order[None, :]).astype(jnp.bfloat16)
    rank = jnp.dot(member.astype(jnp.bfloat16), earlier, preferred_element_type=jnp.float32)
    code = jnp.where(member, rank, -1024.0)
    meta = jnp.concatenate([code, weight], axis=0)
    slots = 2 * INNER * 2 * capacity
    vmem = pl.BlockSpec(memory_space=pltpu.VMEM)
    hbm = pl.BlockSpec(memory_space=pl.ANY)
    quarters = width // 512
    bf16, f32, dma = jnp.bfloat16, jnp.float32, pltpu.SemaphoreType.DMA
    token_grad, grad_in, grad_out = pl.pallas_call(
        functools.partial(fused_kernel, capacity),
        out_shape=[
            jax.ShapeDtypeStruct((count, width), bf16),
            jax.ShapeDtypeStruct((width // 2, 2 * ff), bf16),
            jax.ShapeDtypeStruct((ff, width // 2), bf16),
        ],
        in_specs=[vmem] * 3 + [hbm] * 2,
        out_specs=[vmem, hbm, hbm],
        scratch_shapes=[
            pltpu.VMEM((width, 2 * ff), bf16),
            pltpu.VMEM((ff, width), bf16),
            pltpu.VMEM((width // 2, 2 * ff), bf16),
            pltpu.VMEM((ff, width // 2), bf16),
            pltpu.VMEM((slots // 2, 2 * ff), f32),
            pltpu.VMEM((PLANES, count, width), bf16),
            pltpu.VMEM((PLANES, count, width), bf16),
            pltpu.VMEM((PLANES, 2 * hosts, count), f32),
            pltpu.VMEM((slots, width), bf16),
            pltpu.VMEM((slots, width), bf16),
            pltpu.VMEM((slots, width), bf16),
            pltpu.VMEM((slots, width), bf16),
            pltpu.VMEM((slots, width), bf16),
            pltpu.VMEM((slots, width), bf16),
            pltpu.VMEM((slots, ff), bf16),
            pltpu.VMEM((slots, 2 * ff), bf16),
            pltpu.VMEM((3, count, width), bf16),
            pltpu.VMEM((5, count, width), bf16),
            pltpu.VMEM((count, width), f32),
            pltpu.VMEM((width // 2, 2 * ff), f32),
            pltpu.VMEM((ff, width // 2), f32),
            pltpu.VMEM((width // 2, 2 * ff), f32),
            pltpu.VMEM((ff, width // 2), f32),
            dma((2, 5)),
            dma((2, PLANES)),
            dma((PLANES,)),
            dma((PLANES,)),
            dma((2, 4, INNER)),
            dma((2, 4, INNER)),
            dma((2, INNER, quarters)),
            dma((2, INNER, quarters)),
            dma((3, quarters)),
            dma((5, quarters)),
            dma((2,)),
            dma((2,)),
            dma((4,)),
        ],
        compiler_params=pltpu.CompilerParams(
            collective_id=0, has_side_effects=True, vmem_limit_bytes=60 * 2**20
        ),
        cost_estimate=pl.CostEstimate(
            flops=2 * slots * width * ff * 8, bytes_accessed=12 * 2**20, transcendentals=slots * ff
        ),
    )(tokens, out_grad, meta, w_in[0], w_out[0])
    return token_grad, grad_in[None], grad_out[None]


def body(tokens, out_grad, expert_ids, gate_weights, w_in, w_out):
    hosts = lax.axis_size("expert")
    token_count, model_width = tokens.shape
    capacity = 7 * token_count * expert_ids.shape[1] // (4 * hosts)
    if hosts == 16 and 2 * capacity % 16 == 0:
        return fused(capacity, tokens, out_grad, expert_ids, gate_weights, w_in, w_out)
    pick, slot_weight = selection(
        expert_ids, gate_weights, jnp.arange(hosts, dtype=jnp.int32), capacity
    )
    pick = pick.reshape(hosts * capacity, token_count)
    send_in = jnp.dot(pick, tokens, preferred_element_type=jnp.float32).astype(jnp.bfloat16)
    send_grad = (
        slot_weight.reshape(-1, 1) * jnp.dot(pick, out_grad, preferred_element_type=jnp.float32)
    ).astype(jnp.bfloat16)
    got_in = lax.all_to_all(send_in, "expert", split_axis=0, concat_axis=0, tiled=True)
    got_grad = lax.all_to_all(send_grad, "expert", split_axis=0, concat_axis=0, tiled=True)
    d_rows, grad_in, grad_out = backward_rows(got_in, got_grad, w_in[0], w_out[0])
    returned = lax.all_to_all(d_rows, "expert", split_axis=0, concat_axis=0, tiled=True)
    sum_in = lax.psum_scatter(grad_in, "dp", scatter_dimension=0, tiled=True)
    sum_out = lax.psum_scatter(grad_out, "dp", scatter_dimension=1, tiled=True)
    token_grad = lax.dot_general(
        pick, returned, (((0,), (0,)), ((), ())), preferred_element_type=jnp.float32
    ).astype(jnp.bfloat16)
    return (token_grad, sum_in.astype(jnp.bfloat16)[None], sum_out.astype(jnp.bfloat16)[None])


def solution(mesh):
    in_specs = (
        P(("dp", "expert"), None),
        P(("dp", "expert"), None),
        P(("dp", "expert"), None),
        P(("dp", "expert"), None),
        P("expert", None, None),
        P("expert", None, None),
    )
    out_specs = (P(("dp", "expert"), None), P("expert", "dp", None), P("expert", None, "dp"))
    return jax.shard_map(body, mesh=mesh, in_specs=in_specs, out_specs=out_specs, check_vma=False)
```

```python
import functools
import jax
import jax.numpy as jnp
from jax import lax
from jax.experimental import pallas as pl
from jax.experimental.pallas import tpu as pltpu
from jax.sharding import PartitionSpec as P


def silu_parts(gate_part):
    sigma = 1.0 / (1.0 + jnp.exp(-gate_part))
    return (gate_part * sigma, sigma * (1.0 + gate_part * (1.0 - sigma)))


def backward_rows(rows_in, rows_grad, weight_in, weight_out):
    hidden_width = weight_out.shape[0]
    joined = jnp.dot(rows_in, weight_in, preferred_element_type=jnp.float32)
    gate_part = joined[:, :hidden_width]
    up_part = joined[:, hidden_width:]
    activated, derivative = silu_parts(gate_part)
    hidden = (activated * up_part).astype(jnp.bfloat16)
    d_hidden = lax.dot_general(
        rows_grad, weight_out, (((1,), (1,)), ((), ())), preferred_element_type=jnp.float32
    )
    d_joined = jnp.concatenate(
        [d_hidden * up_part * derivative, d_hidden * activated], axis=1
    ).astype(jnp.bfloat16)
    d_rows = lax.dot_general(
        d_joined, weight_in, (((1,), (1,)), ((), ())), preferred_element_type=jnp.float32
    ).astype(jnp.bfloat16)
    grad_in = lax.dot_general(
        rows_in, d_joined, (((0,), (0,)), ((), ())), preferred_element_type=jnp.float32
    )
    grad_out = lax.dot_general(
        hidden, rows_grad, (((0,), (0,)), ((), ())), preferred_element_type=jnp.float32
    )
    return (d_rows, grad_in, grad_out)


def selection(ids, weights, experts, capacity):
    count = ids.shape[0]
    hit = ids[:, :, None] == experts[None, None, :]
    member = jnp.any(hit, axis=1)
    weight = jnp.sum(jnp.where(hit, weights[:, :, None], 0.0), axis=1)
    earlier = (
        jnp.arange(count, dtype=jnp.int32)[:, None] > jnp.arange(count, dtype=jnp.int32)[None, :]
    ).astype(jnp.bfloat16)
    rank = jnp.dot(earlier, member.astype(jnp.bfloat16), preferred_element_type=jnp.float32)
    rank = jnp.where(member, rank.astype(jnp.int32), -1)
    chosen = rank.T[:, None, :] == jnp.arange(capacity, dtype=jnp.int32)[None, :, None]
    slot_weight = jnp.sum(jnp.where(chosen, weight.T[:, None, :], 0.0), axis=2)
    return chosen.astype(jnp.bfloat16), slot_weight


PLANES = 4
INNER = 4
MESH = pl.DeviceIdType.MESH


def flipped(p, d):
    x, y = p % 2, p // 2
    if d % 2:
        x = 1 - x
    if d // 2:
        y = 1 - y
    return 2 * y + x


def fused_kernel(
    capacity,
    tok_ref,
    og_ref,
    meta_ref,
    w_in_hbm,
    w_out_hbm,
    tg_ref,
    gin_hbm,
    gout_hbm,
    w_in_ref,
    w_out_ref,
    gin_ref,
    gout_ref,
    joined_ref,
    ztok,
    zog,
    zmeta,
    send_in,
    send_gr,
    got_in,
    got_gr,
    d_rows,
    ret,
    hid,
    dj,
    part,
    part_got,
    kept,
    peer_in,
    peer_out,
    far_in,
    far_out,
    z_send,
    z_recv,
    meta_send,
    meta_recv,
    p_send,
    p_recv,
    r_send,
    r_recv,
    t_send,
    t_recv,
    g_send,
    g_recv,
    local_sem,
):
    me = lax.axis_index("expert")
    core = lax.axis_index("dp")
    z, p = me // INNER, me % INNER
    count, width = tok_ref.shape
    ff = w_out_ref.shape[0]
    rows = 2 * capacity
    block_rows = INNER * rows
    wide = 512
    odd = z % 2
    pair = z // 2
    partner = z + 1 - 2 * odd
    is_inner = jnp.logical_or(z == 1, z == 2)
    near = 2 - pair
    far = 3 * (1 - pair)
    zdev = lambda s: {"expert": s * INNER + p}
    pdev = lambda d: {"expert": z * INNER + flipped(p, d)}

    def remote(src, dst, send_sem, recv_sem, device):
        return pltpu.make_async_remote_copy(
            src_ref=src,
            dst_ref=dst,
            send_sem=send_sem,
            recv_sem=recv_sem,
            device_id=device,
            device_id_type=MESH,
        )

    loads = [
        pltpu.make_async_copy(w_in_hbm, w_in_ref, local_sem.at[0]),
        pltpu.make_async_copy(w_out_hbm, w_out_ref, local_sem.at[1]),
    ]
    stores = [
        pltpu.make_async_copy(gin_ref, gin_hbm, local_sem.at[2]),
        pltpu.make_async_copy(gout_ref, gout_hbm, local_sem.at[3]),
    ]
    barrier = pltpu.get_barrier_semaphore()
    for k in range(1, PLANES):
        pl.semaphore_signal(barrier, inc=1, device_id=zdev((z + k) % PLANES), device_id_type=MESH)
    for d in range(1, INNER):
        pl.semaphore_signal(barrier, inc=1, device_id=pdev(d), device_id_type=MESH)
    pl.semaphore_signal(barrier, inc=1, device_id={"dp": 1 - core}, device_id_type=MESH)
    pl.semaphore_wait(barrier, PLANES + INNER - 1)

    held = (ztok, zog)
    own = (tok_ref, og_ref)

    def meta_copy(s):
        return remote(meta_ref, zmeta.at[z], meta_send.at[s], meta_recv.at[z], zdev(s))

    def arrive_meta(s):
        remote(meta_ref, zmeta.at[s], meta_send.at[s], meta_recv.at[s], zdev(s)).wait_recv()

    def own_copy(a, k, to):
        return remote(own[a], held[a].at[z], z_send.at[a, k], z_recv.at[a, z], zdev(to))

    def pass_on(a, k, s, to):
        return remote(held[a].at[s], held[a].at[s], z_send.at[a, k], z_recv.at[a, s], zdev(to))

    def arrive(a, s):
        remote(held[a].at[s], held[a].at[s], z_send.at[a, 0], z_recv.at[a, s], zdev(s)).wait_recv()

    others = [(z + k) % PLANES for k in range(1, PLANES)]
    cross = near
    for s in others:
        meta_copy(s).start()
    for a in range(2):
        own_copy(a, 0, partner).start()

        @pl.when(is_inner)
        def _():
            own_copy(a, 1, cross).start()

    for copy in loads:
        copy.start()
    ztok[z] = tok_ref[...]
    zog[z] = og_ref[...]
    zmeta[z] = meta_ref[...]

    row_id = lax.broadcasted_iota(jnp.int32, (rows, count), 0).astype(jnp.float32)

    def planes_of(b):
        return (z, partner) if b == 0 else (near, far)

    def chosen(s, half, d):
        expert = z * INNER + flipped(p, d)
        code = zmeta[s, pl.ds(expert, 1), :]
        return row_id == code + float(half * capacity)

    ready = capacity // 16 * 16
    pieces = tuple((b, *cut) for b in range(2) for cut in ((0, ready), (ready, rows - ready)))

    def plane_copy(a, piece, d):
        b, start, size = pieces[piece]
        src = (send_in, send_gr)[a]
        dst = (got_in, got_gr)[a]
        at = pl.ds(b * block_rows + d * rows + start, size)
        return remote(
            src.at[at], dst.at[at], p_send.at[a, piece, d], p_recv.at[a, piece, d], pdev(d)
        )

    def dispatch(a, piece):
        b, start, size = pieces[piece]
        planes = planes_of(b)[: 1 if start == 0 else 2]
        for d in (3, 1, 2, 0):
            picks = [chosen(s, half, d)[start : start + size] for half, s in enumerate(planes)]
            sels = [pick.astype(jnp.bfloat16) for pick in picks]
            if a == 1:
                expert = z * INNER + flipped(p, d) + PLANES * INNER
                scale = jnp.sum(
                    sum(
                        jnp.where(pick, zmeta[s, pl.ds(expert, 1), :], 0.0)
                        for pick, s in zip(picks, planes)
                    ),
                    axis=1,
                    keepdims=True,
                )
            out = ((got_in, got_gr) if d == 0 else (send_in, send_gr))[a]
            at = pl.ds(b * block_rows + d * rows + start, size)

            @pl.loop(0, width // wide)
            def _(c):
                cols = pl.ds(pl.multiple_of(c * wide, wide), wide)
                picked = sum(
                    jnp.dot(sel, held[a][s, :, cols], preferred_element_type=jnp.float32)
                    for sel, s in zip(sels, planes)
                )
                if a == 1:
                    picked = picked * scale
                out[at, cols] = picked.astype(jnp.bfloat16)

            if d:
                plane_copy(a, piece, d).start()

    dispatch(0, 0)
    dispatch(1, 0)

    arrive(0, partner)

    @pl.when(is_inner)
    def _():
        pass_on(0, 2, partner, cross).start()

    arrive_meta(partner)
    dispatch(0, 1)
    arrive(1, partner)

    @pl.when(is_inner)
    def _():
        pass_on(1, 2, partner, cross).start()
        for a in range(2):
            arrive(a, near)
            pass_on(a, 3, near, partner).start()

    dispatch(1, 1)

    arrive_meta(near)
    arrive_meta(far)
    for a in range(2):

        @pl.when(jnp.logical_not(is_inner))
        def _():
            arrive(a, near)

        dispatch(a, 2)

        if a == 0:

            @pl.when(is_inner)
            def _():
                for other in range(2):
                    arrive(other, far)
                    pass_on(other, 4, far, partner).start()

    def arrive_rows(a, b):
        for d in range(1, INNER):
            for piece in range(len(pieces)):
                if pieces[piece][0] == b:
                    plane_copy(a, piece, d).wait_recv()

    tile_rows = block_rows // 2
    quarters = width // wide

    def joined_rows(b):
        @pl.loop(0, 2)
        def _(t):
            at = pl.ds(pl.multiple_of(b * block_rows + t * tile_rows, 16), tile_rows)
            joined_ref[pl.ds(pl.multiple_of(t * tile_rows, 16), tile_rows), :] = jnp.dot(
                got_in[at, :], w_in_ref[...], preferred_element_type=jnp.float32
            )

    def hidden_rows(b):
        @pl.loop(0, 2)
        def _(t):
            at = pl.ds(pl.multiple_of(b * block_rows + t * tile_rows, 16), tile_rows)
            here = pl.ds(pl.multiple_of(t * tile_rows, 16), tile_rows)
            gate_part, up_part = joined_ref[here, :ff], joined_ref[here, ff:]
            activated, derivative = silu_parts(gate_part)
            hid[at, :] = (activated * up_part).astype(jnp.bfloat16)
            d_hidden = lax.dot_general(
                got_gr[at, :],
                w_out_ref[...],
                (((1,), (1,)), ((), ())),
                preferred_element_type=jnp.float32,
            )
            dj[at, :ff] = (d_hidden * up_part * derivative).astype(jnp.bfloat16)
            dj[at, ff:] = (d_hidden * activated).astype(jnp.bfloat16)

    def input_rows(b, c):
        at = pl.ds(b * block_rows, block_rows)
        cols = pl.ds(c * wide, wide)
        d_rows[at, cols] = lax.dot_general(
            dj[at, :],
            w_in_ref[cols, :],
            (((1,), (1,)), ((), ())),
            preferred_element_type=jnp.float32,
        ).astype(jnp.bfloat16)

    def back_copy(b, d, c):
        at = (pl.ds(b * block_rows + d * rows, rows), pl.ds(c * wide, wide))
        return remote(d_rows.at[at], ret.at[at], r_send.at[b, d, c], r_recv.at[b, d, c], pdev(d))

    from_end_near, from_end_far, from_partner, from_cross, from_cross_far = range(5)

    def part_copy(slot, land, to, c):
        cols = pl.ds(c * wide, wide)
        return remote(
            part.at[slot, :, cols],
            part_got.at[land, :, cols],
            t_send.at[slot, c],
            t_recv.at[land, c],
            zdev(to),
        )

    def landed(land, c):
        cols = pl.ds(c * wide, wide)
        part_copy(0, land, partner, c).wait_recv()
        return part_got[land, :, cols].astype(jnp.float32)

    def send_part(total, slot, land, to, c):
        part[slot, :, pl.ds(c * wide, wide)] = total.astype(jnp.bfloat16)
        part_copy(slot, land, to, c).start()

    def combine(b, half, c):
        s = planes_of(b)[half]
        cols = pl.ds(c * wide, wide)
        total = jnp.zeros((count, wide), jnp.float32)
        for d in range(INNER):
            at = pl.ds(b * block_rows + d * rows, rows)
            total = total + lax.dot_general(
                chosen(s, half, d).astype(jnp.bfloat16),
                (ret if d else d_rows)[at, cols],
                (((0,), (0,)), ((), ())),
                preferred_element_type=jnp.float32,
            )
        return total

    for copy in loads:
        copy.wait()
    arrive_rows(0, 0)
    joined_rows(0)
    arrive_rows(1, 0)
    hidden_rows(0)
    for c in range(quarters):
        input_rows(0, c)

    for a in range(2):

        @pl.when(jnp.logical_not(is_inner))
        def _():
            arrive(a, far)

        dispatch(a, 3)

    early = ((3, 0), (3, 1))
    arrive_rows(0, 1)
    joined_rows(1)
    arrive_rows(1, 1)
    for d, c in early:
        back_copy(0, d, c).start()
    hidden_rows(1)
    for c in range(quarters):
        input_rows(1, c)
        for d in (3, 1, 2):
            back_copy(1, d, c).start()

    half_width = width // 2
    tile = 256

    def weight_tiles(cols):
        to_in = lax.dot_general(
            got_in[:, cols], dj[...], (((0,), (0,)), ((), ())), preferred_element_type=jnp.float32
        )
        to_out = lax.dot_general(
            hid[...], got_gr[:, cols], (((0,), (0,)), ((), ())), preferred_element_type=jnp.float32
        )
        return to_in, to_out

    @pl.loop(0, half_width // tile)
    def _(c):
        at = pl.ds(pl.multiple_of(c * tile, tile), tile)
        cols = pl.ds(pl.multiple_of((1 - core) * half_width + c * tile, tile), tile)
        to_in, to_out = weight_tiles(cols)
        peer_in[at, :] = to_in
        peer_out[:, at] = to_out

    swaps = [
        remote(peer_in, far_in, g_send.at[0], g_recv.at[0], {"dp": 1 - core}),
        remote(peer_out, far_out, g_send.at[1], g_recv.at[1], {"dp": 1 - core}),
    ]
    for copy in swaps:
        copy.start()

    for c in range(quarters):
        for d in range(1, INNER):
            back_copy(1, d, c).wait_recv()
        for d in (3, 1, 2):
            if (d, c) not in early:
                back_copy(0, d, c).start()
        totals = [combine(1, half, c) for half in range(2)]

        @pl.when(is_inner)
        def _():
            for k in range(2):
                send_part(totals[k] + landed(from_end_near + k, c), k, from_cross + k, near, c)

        @pl.when(jnp.logical_not(is_inner))
        def _():
            for k in range(2):
                send_part(totals[k], k, from_end_near + k, partner, c)

    for copy in swaps:
        copy.wait_recv()

    @pl.loop(0, half_width // tile)
    def _(c):
        at = pl.ds(pl.multiple_of(c * tile, tile), tile)
        cols = pl.ds(pl.multiple_of(core * half_width + c * tile, tile), tile)
        to_in, to_out = weight_tiles(cols)
        gin_ref[at, :] = (to_in + far_in[at, :]).astype(jnp.bfloat16)
        gout_ref[:, at] = (to_out + far_out[:, at]).astype(jnp.bfloat16)

    for copy in stores:
        copy.start()

    for c in range(quarters):
        for d in range(1, INNER):
            back_copy(0, d, c).wait_recv()
        total = combine(0, 1, c)

        @pl.when(is_inner)
        def _():
            send_part(total + landed(from_cross_far, c), 2, from_partner, partner, c)

        @pl.when(jnp.logical_not(is_inner))
        def _():
            send_part(total, 2, from_partner, partner, c)

        kept[:, pl.ds(c * wide, wide)] = combine(0, 0, c)

    for c in range(quarters):
        cols = pl.ds(c * wide, wide)
        kept[:, cols] += landed(from_partner, c)

        @pl.when(is_inner)
        def _():
            kept[:, cols] += landed(from_cross, c)

        tg_ref[:, cols] = kept[:, cols].astype(jnp.bfloat16)

    for s in others:
        meta_copy(s).wait_send()
    for slot in range(3):
        for c in range(quarters):
            part_copy(slot, from_partner, partner, c).wait_send()
    for a in range(2):
        own_copy(a, 0, partner).wait_send()

        @pl.when(is_inner)
        def _():
            own_copy(a, 1, cross).wait_send()
            pass_on(a, 2, partner, cross).wait_send()
            pass_on(a, 3, near, partner).wait_send()
            pass_on(a, 4, far, partner).wait_send()

    for d in range(1, INNER):
        for a in range(2):
            for piece in range(len(pieces)):
                plane_copy(a, piece, d).wait_send()
        for b in range(2):
            for c in range(quarters):
                back_copy(b, d, c).wait_send()
    for copy in swaps:
        copy.wait_send()
    for copy in stores:
        copy.wait()


def settle_kernel(parts, *refs):
    held, given, sems = refs[: len(refs) // 2], refs[len(refs) // 2 : -1], refs[-1]
    copies = []
    for k, (src, dst) in enumerate(zip(held, given)):
        size = src.shape[0] // parts
        for i in range(parts):
            at = pl.ds(i * size, size)
            copies.append(pltpu.make_async_copy(src.at[at], dst.at[at], sems.at[k, i]))
    for copy in copies:
        copy.start()
    for copy in copies:
        copy.wait()


def settle(*arrays):
    parts = 4
    hbm = pl.BlockSpec(memory_space=pl.ANY)
    return pl.pallas_call(
        functools.partial(settle_kernel, parts),
        out_shape=[jax.ShapeDtypeStruct(a.shape, a.dtype) for a in arrays],
        in_specs=[hbm] * len(arrays),
        out_specs=[hbm] * len(arrays),
        scratch_shapes=[pltpu.SemaphoreType.DMA((len(arrays), parts))],
    )(*arrays)


def fused(capacity, tokens, out_grad, expert_ids, gate_weights, w_in, w_out):
    hosts = PLANES * INNER
    count, width = tokens.shape
    ff = w_out.shape[1]
    hit = expert_ids.T[:, None, :] == jnp.arange(hosts, dtype=jnp.int32)[None, :, None]
    member = jnp.any(hit, axis=0)
    weight = jnp.sum(jnp.where(hit, gate_weights.T[:, None, :], 0.0), axis=0)
    order = jnp.arange(count, dtype=jnp.int32)
    earlier = (order[:, None] < order[None, :]).astype(jnp.bfloat16)
    rank = jnp.dot(member.astype(jnp.bfloat16), earlier, preferred_element_type=jnp.float32)
    code = jnp.where(member, rank, -1024.0)
    meta = jnp.concatenate([code, weight], axis=0)
    slots = 2 * INNER * 2 * capacity
    vmem = pl.BlockSpec(memory_space=pltpu.VMEM)
    hbm = pl.BlockSpec(memory_space=pl.ANY)
    quarters = width // 512
    bf16, f32, dma = jnp.bfloat16, jnp.float32, pltpu.SemaphoreType.DMA
    token_grad, grad_in, grad_out = pl.pallas_call(
        functools.partial(fused_kernel, capacity),
        out_shape=[
            jax.ShapeDtypeStruct((count, width), bf16),
            jax.ShapeDtypeStruct((width // 2, 2 * ff), bf16),
            jax.ShapeDtypeStruct((ff, width // 2), bf16),
        ],
        in_specs=[vmem] * 3 + [hbm] * 2,
        out_specs=[vmem, hbm, hbm],
        scratch_shapes=[
            pltpu.VMEM((width, 2 * ff), bf16),
            pltpu.VMEM((ff, width), bf16),
            pltpu.VMEM((width // 2, 2 * ff), bf16),
            pltpu.VMEM((ff, width // 2), bf16),
            pltpu.VMEM((slots // 2, 2 * ff), f32),
            pltpu.VMEM((PLANES, count, width), bf16),
            pltpu.VMEM((PLANES, count, width), bf16),
            pltpu.VMEM((PLANES, 2 * hosts, count), f32),
            pltpu.VMEM((slots, width), bf16),
            pltpu.VMEM((slots, width), bf16),
            pltpu.VMEM((slots, width), bf16),
            pltpu.VMEM((slots, width), bf16),
            pltpu.VMEM((slots, width), bf16),
            pltpu.VMEM((slots, width), bf16),
            pltpu.VMEM((slots, ff), bf16),
            pltpu.VMEM((slots, 2 * ff), bf16),
            pltpu.VMEM((3, count, width), bf16),
            pltpu.VMEM((5, count, width), bf16),
            pltpu.VMEM((count, width), f32),
            pltpu.VMEM((width // 2, 2 * ff), f32),
            pltpu.VMEM((ff, width // 2), f32),
            pltpu.VMEM((width // 2, 2 * ff), f32),
            pltpu.VMEM((ff, width // 2), f32),
            dma((2, 5)),
            dma((2, PLANES)),
            dma((PLANES,)),
            dma((PLANES,)),
            dma((2, 4, INNER)),
            dma((2, 4, INNER)),
            dma((2, INNER, quarters)),
            dma((2, INNER, quarters)),
            dma((3, quarters)),
            dma((5, quarters)),
            dma((2,)),
            dma((2,)),
            dma((4,)),
        ],
        compiler_params=pltpu.CompilerParams(
            collective_id=0, has_side_effects=True, vmem_limit_bytes=60 * 2**20
        ),
        cost_estimate=pl.CostEstimate(
            flops=2 * slots * width * ff * 8, bytes_accessed=12 * 2**20, transcendentals=slots * ff
        ),
    )(tokens, out_grad, meta, w_in[0], w_out[0])
    token_grad, grad_in, grad_out = settle(token_grad, grad_in, grad_out)
    return token_grad, grad_in[None], grad_out[None]


def body(tokens, out_grad, expert_ids, gate_weights, w_in, w_out):
    hosts = lax.axis_size("expert")
    token_count, model_width = tokens.shape
    capacity = 7 * token_count * expert_ids.shape[1] // (4 * hosts)
    if hosts == 16 and 2 * capacity % 16 == 0:
        return fused(capacity, tokens, out_grad, expert_ids, gate_weights, w_in, w_out)
    pick, slot_weight = selection(
        expert_ids, gate_weights, jnp.arange(hosts, dtype=jnp.int32), capacity
    )
    pick = pick.reshape(hosts * capacity, token_count)
    send_in = jnp.dot(pick, tokens, preferred_element_type=jnp.float32).astype(jnp.bfloat16)
    send_grad = (
        slot_weight.reshape(-1, 1) * jnp.dot(pick, out_grad, preferred_element_type=jnp.float32)
    ).astype(jnp.bfloat16)
    got_in = lax.all_to_all(send_in, "expert", split_axis=0, concat_axis=0, tiled=True)
    got_grad = lax.all_to_all(send_grad, "expert", split_axis=0, concat_axis=0, tiled=True)
    d_rows, grad_in, grad_out = backward_rows(got_in, got_grad, w_in[0], w_out[0])
    returned = lax.all_to_all(d_rows, "expert", split_axis=0, concat_axis=0, tiled=True)
    sum_in = lax.psum_scatter(grad_in, "dp", scatter_dimension=0, tiled=True)
    sum_out = lax.psum_scatter(grad_out, "dp", scatter_dimension=1, tiled=True)
    token_grad = lax.dot_general(
        pick, returned, (((0,), (0,)), ((), ())), preferred_element_type=jnp.float32
    ).astype(jnp.bfloat16)
    return (token_grad, sum_in.astype(jnp.bfloat16)[None], sum_out.astype(jnp.bfloat16)[None])


def solution(mesh):
    in_specs = (
        P(("dp", "expert"), None),
        P(("dp", "expert"), None),
        P(("dp", "expert"), None),
        P(("dp", "expert"), None),
        P("expert", None, None),
        P("expert", None, None),
    )
    out_specs = (P(("dp", "expert"), None), P("expert", "dp", None), P("expert", None, "dp"))
    return jax.shard_map(body, mesh=mesh, in_specs=in_specs, out_specs=out_specs, check_vma=False)
```

```python
import functools
import jax
import jax.numpy as jnp
from jax import lax
from jax.experimental import pallas as pl
from jax.experimental.pallas import tpu as pltpu
from jax.sharding import PartitionSpec as P


def silu_parts(gate_part):
    sigma = 1.0 / (1.0 + jnp.exp(-gate_part))
    return (gate_part * sigma, sigma * (1.0 + gate_part * (1.0 - sigma)))


def backward_rows(rows_in, rows_grad, weight_in, weight_out):
    hidden_width = weight_out.shape[0]
    joined = jnp.dot(rows_in, weight_in, preferred_element_type=jnp.float32)
    gate_part = joined[:, :hidden_width]
    up_part = joined[:, hidden_width:]
    activated, derivative = silu_parts(gate_part)
    hidden = (activated * up_part).astype(jnp.bfloat16)
    d_hidden = lax.dot_general(
        rows_grad, weight_out, (((1,), (1,)), ((), ())), preferred_element_type=jnp.float32
    )
    d_joined = jnp.concatenate(
        [d_hidden * up_part * derivative, d_hidden * activated], axis=1
    ).astype(jnp.bfloat16)
    d_rows = lax.dot_general(
        d_joined, weight_in, (((1,), (1,)), ((), ())), preferred_element_type=jnp.float32
    ).astype(jnp.bfloat16)
    grad_in = lax.dot_general(
        rows_in, d_joined, (((0,), (0,)), ((), ())), preferred_element_type=jnp.float32
    )
    grad_out = lax.dot_general(
        hidden, rows_grad, (((0,), (0,)), ((), ())), preferred_element_type=jnp.float32
    )
    return (d_rows, grad_in, grad_out)


def selection(ids, weights, experts, capacity):
    count = ids.shape[0]
    hit = ids[:, :, None] == experts[None, None, :]
    member = jnp.any(hit, axis=1)
    weight = jnp.sum(jnp.where(hit, weights[:, :, None], 0.0), axis=1)
    earlier = (
        jnp.arange(count, dtype=jnp.int32)[:, None] > jnp.arange(count, dtype=jnp.int32)[None, :]
    ).astype(jnp.bfloat16)
    rank = jnp.dot(earlier, member.astype(jnp.bfloat16), preferred_element_type=jnp.float32)
    rank = jnp.where(member, rank.astype(jnp.int32), -1)
    chosen = rank.T[:, None, :] == jnp.arange(capacity, dtype=jnp.int32)[None, :, None]
    slot_weight = jnp.sum(jnp.where(chosen, weight.T[:, None, :], 0.0), axis=2)
    return chosen.astype(jnp.bfloat16), slot_weight


PLANES = 4
INNER = 4
MESH = pl.DeviceIdType.MESH


def flipped(p, d):
    x, y = p % 2, p // 2
    if d % 2:
        x = 1 - x
    if d // 2:
        y = 1 - y
    return 2 * y + x


def fused_kernel(
    capacity,
    tok_ref,
    og_ref,
    meta_ref,
    w_in_hbm,
    w_out_hbm,
    tg_ref,
    gin_hbm,
    gout_hbm,
    w_in_ref,
    w_out_ref,
    gin_ref,
    gout_ref,
    joined_ref,
    ztok,
    zog,
    zmeta,
    send_in,
    send_gr,
    got_in,
    got_gr,
    d_rows,
    ret,
    hid,
    dj,
    part,
    part_got,
    kept,
    peer_in,
    peer_out,
    far_in,
    far_out,
    z_send,
    z_recv,
    meta_send,
    meta_recv,
    p_send,
    p_recv,
    r_send,
    r_recv,
    t_send,
    t_recv,
    g_send,
    g_recv,
    local_sem,
):
    me = lax.axis_index("expert")
    core = lax.axis_index("dp")
    z, p = me // INNER, me % INNER
    count, width = tok_ref.shape
    ff = w_out_ref.shape[0]
    rows = 2 * capacity
    block_rows = INNER * rows
    wide = 512
    odd = z % 2
    pair = z // 2
    partner = z + 1 - 2 * odd
    is_inner = jnp.logical_or(z == 1, z == 2)
    near = 2 - pair
    far = 3 * (1 - pair)
    zdev = lambda s: {"expert": s * INNER + p}
    pdev = lambda d: {"expert": z * INNER + flipped(p, d)}

    def remote(src, dst, send_sem, recv_sem, device):
        return pltpu.make_async_remote_copy(
            src_ref=src,
            dst_ref=dst,
            send_sem=send_sem,
            recv_sem=recv_sem,
            device_id=device,
            device_id_type=MESH,
        )

    loads = [
        pltpu.make_async_copy(w_in_hbm, w_in_ref, local_sem.at[0]),
        pltpu.make_async_copy(w_out_hbm, w_out_ref, local_sem.at[1]),
    ]
    stores = [
        pltpu.make_async_copy(gin_ref, gin_hbm, local_sem.at[2]),
        pltpu.make_async_copy(gout_ref, gout_hbm, local_sem.at[3]),
    ]
    barrier = pltpu.get_barrier_semaphore()
    for k in range(1, PLANES):
        pl.semaphore_signal(barrier, inc=1, device_id=zdev((z + k) % PLANES), device_id_type=MESH)
    for d in range(1, INNER):
        pl.semaphore_signal(barrier, inc=1, device_id=pdev(d), device_id_type=MESH)
    pl.semaphore_signal(barrier, inc=1, device_id={"dp": 1 - core}, device_id_type=MESH)
    pl.semaphore_wait(barrier, PLANES + INNER - 1)

    held = (ztok, zog)
    own = (tok_ref, og_ref)

    def meta_copy(s):
        return remote(meta_ref, zmeta.at[z], meta_send.at[s], meta_recv.at[z], zdev(s))

    def arrive_meta(s):
        remote(meta_ref, zmeta.at[s], meta_send.at[s], meta_recv.at[s], zdev(s)).wait_recv()

    def own_copy(a, k, to):
        return remote(own[a], held[a].at[z], z_send.at[a, k], z_recv.at[a, z], zdev(to))

    def pass_on(a, k, s, to):
        return remote(held[a].at[s], held[a].at[s], z_send.at[a, k], z_recv.at[a, s], zdev(to))

    def arrive(a, s):
        remote(held[a].at[s], held[a].at[s], z_send.at[a, 0], z_recv.at[a, s], zdev(s)).wait_recv()

    others = [(z + k) % PLANES for k in range(1, PLANES)]
    cross = near
    for s in others:
        meta_copy(s).start()
    for a in range(2):
        own_copy(a, 0, partner).start()

        @pl.when(is_inner)
        def _():
            own_copy(a, 1, cross).start()

    for copy in loads:
        copy.start()
    ztok[z] = tok_ref[...]
    zog[z] = og_ref[...]
    zmeta[z] = meta_ref[...]

    row_id = lax.broadcasted_iota(jnp.int32, (rows, count), 0).astype(jnp.float32)

    def planes_of(b):
        return (z, partner) if b == 0 else (near, far)

    def chosen(s, half, d):
        expert = z * INNER + flipped(p, d)
        code = zmeta[s, pl.ds(expert, 1), :]
        return row_id == code + float(half * capacity)

    ready = capacity // 16 * 16
    pieces = tuple((b, *cut) for b in range(2) for cut in ((0, ready), (ready, rows - ready)))

    def plane_copy(a, piece, d):
        b, start, size = pieces[piece]
        src = (send_in, send_gr)[a]
        dst = (got_in, got_gr)[a]
        at = pl.ds(b * block_rows + d * rows + start, size)
        return remote(
            src.at[at], dst.at[at], p_send.at[a, piece, d], p_recv.at[a, piece, d], pdev(d)
        )

    def dispatch(a, piece):
        b, start, size = pieces[piece]
        planes = planes_of(b)[: 1 if start == 0 else 2]
        for d in (3, 1, 2, 0):
            picks = [chosen(s, half, d)[start : start + size] for half, s in enumerate(planes)]
            sels = [pick.astype(jnp.bfloat16) for pick in picks]
            if a == 1:
                expert = z * INNER + flipped(p, d) + PLANES * INNER
                scale = jnp.sum(
                    sum(
                        jnp.where(pick, zmeta[s, pl.ds(expert, 1), :], 0.0)
                        for pick, s in zip(picks, planes)
                    ),
                    axis=1,
                    keepdims=True,
                )
            out = ((got_in, got_gr) if d == 0 else (send_in, send_gr))[a]
            at = pl.ds(b * block_rows + d * rows + start, size)

            @pl.loop(0, width // wide)
            def _(c):
                cols = pl.ds(pl.multiple_of(c * wide, wide), wide)
                picked = sum(
                    jnp.dot(sel, held[a][s, :, cols], preferred_element_type=jnp.float32)
                    for sel, s in zip(sels, planes)
                )
                if a == 1:
                    picked = picked * scale
                out[at, cols] = picked.astype(jnp.bfloat16)

            if d:
                plane_copy(a, piece, d).start()

    dispatch(0, 0)
    dispatch(1, 0)

    arrive(0, partner)

    @pl.when(is_inner)
    def _():
        pass_on(0, 2, partner, cross).start()

    arrive_meta(partner)
    dispatch(0, 1)
    arrive(1, partner)

    @pl.when(is_inner)
    def _():
        pass_on(1, 2, partner, cross).start()
        for a in range(2):
            arrive(a, near)
            pass_on(a, 3, near, partner).start()

    dispatch(1, 1)

    arrive_meta(near)
    arrive_meta(far)
    for a in range(2):

        @pl.when(jnp.logical_not(is_inner))
        def _():
            arrive(a, near)

        dispatch(a, 2)

        if a == 0:

            @pl.when(is_inner)
            def _():
                for other in range(2):
                    arrive(other, far)
                    pass_on(other, 4, far, partner).start()

    def arrive_rows(a, b):
        for d in range(1, INNER):
            for piece in range(len(pieces)):
                if pieces[piece][0] == b:
                    plane_copy(a, piece, d).wait_recv()

    tile_rows = block_rows // 2
    quarters = width // wide

    def joined_rows(b):
        @pl.loop(0, 2)
        def _(t):
            at = pl.ds(pl.multiple_of(b * block_rows + t * tile_rows, 16), tile_rows)
            joined_ref[pl.ds(pl.multiple_of(t * tile_rows, 16), tile_rows), :] = jnp.dot(
                got_in[at, :], w_in_ref[...], preferred_element_type=jnp.float32
            )

    def hidden_rows(b):
        @pl.loop(0, 2)
        def _(t):
            at = pl.ds(pl.multiple_of(b * block_rows + t * tile_rows, 16), tile_rows)
            here = pl.ds(pl.multiple_of(t * tile_rows, 16), tile_rows)
            gate_part, up_part = joined_ref[here, :ff], joined_ref[here, ff:]
            activated, derivative = silu_parts(gate_part)
            hid[at, :] = (activated * up_part).astype(jnp.bfloat16)
            d_hidden = lax.dot_general(
                got_gr[at, :],
                w_out_ref[...],
                (((1,), (1,)), ((), ())),
                preferred_element_type=jnp.float32,
            )
            dj[at, :ff] = (d_hidden * up_part * derivative).astype(jnp.bfloat16)
            dj[at, ff:] = (d_hidden * activated).astype(jnp.bfloat16)

    def input_rows(b, c):
        at = pl.ds(b * block_rows, block_rows)
        cols = pl.ds(c * wide, wide)
        d_rows[at, cols] = lax.dot_general(
            dj[at, :],
            w_in_ref[cols, :],
            (((1,), (1,)), ((), ())),
            preferred_element_type=jnp.float32,
        ).astype(jnp.bfloat16)

    back_own, back_pair, back_far = range(3)

    def back_copy(piece, d, c):
        b, start, size = ((0, 0, ready), (0, ready, rows - ready), (1, 0, rows))[piece]
        at = (pl.ds(b * block_rows + d * rows + start, size), pl.ds(c * wide, wide))
        return remote(
            d_rows.at[at], ret.at[at], r_send.at[piece, d, c], r_recv.at[piece, d, c], pdev(d)
        )

    from_end_near, from_end_far, from_partner, from_cross, from_cross_far = range(5)

    def part_copy(slot, land, to, c):
        cols = pl.ds(c * wide, wide)
        return remote(
            part.at[slot, :, cols],
            part_got.at[land, :, cols],
            t_send.at[slot, c],
            t_recv.at[land, c],
            zdev(to),
        )

    def landed(land, c):
        cols = pl.ds(c * wide, wide)
        part_copy(0, land, partner, c).wait_recv()
        return part_got[land, :, cols].astype(jnp.float32)

    def send_part(total, slot, land, to, c):
        part[slot, :, pl.ds(c * wide, wide)] = total.astype(jnp.bfloat16)
        part_copy(slot, land, to, c).start()

    def combine(b, half, c):
        s = planes_of(b)[half]
        cols = pl.ds(c * wide, wide)
        total = jnp.zeros((count, wide), jnp.float32)
        for d in range(INNER):
            start = ready if (b, half) == (0, 1) else 0
            at = pl.ds(b * block_rows + d * rows + start, rows - start)
            total = total + lax.dot_general(
                chosen(s, half, d)[start:].astype(jnp.bfloat16),
                (ret if d else d_rows)[at, cols],
                (((0,), (0,)), ((), ())),
                preferred_element_type=jnp.float32,
            )
        return total

    for copy in loads:
        copy.wait()
    arrive_rows(0, 0)
    joined_rows(0)
    arrive_rows(1, 0)
    hidden_rows(0)
    for c in range(quarters):
        input_rows(0, c)

    for a in range(2):

        @pl.when(jnp.logical_not(is_inner))
        def _():
            arrive(a, far)

        dispatch(a, 3)

    early = ((3, 0), (3, 1))
    arrive_rows(0, 1)
    joined_rows(1)
    arrive_rows(1, 1)
    for d, c in early:
        back_copy(back_pair, d, c).start()
    hidden_rows(1)
    for c in range(quarters):
        input_rows(1, c)
        for d in (3, 1, 2):
            back_copy(back_far, d, c).start()

    half_width = width // 2
    tile = 256

    def weight_tiles(cols):
        to_in = lax.dot_general(
            got_in[:, cols], dj[...], (((0,), (0,)), ((), ())), preferred_element_type=jnp.float32
        )
        to_out = lax.dot_general(
            hid[...], got_gr[:, cols], (((0,), (0,)), ((), ())), preferred_element_type=jnp.float32
        )
        return to_in, to_out

    @pl.loop(0, half_width // tile)
    def _(c):
        at = pl.ds(pl.multiple_of(c * tile, tile), tile)
        cols = pl.ds(pl.multiple_of((1 - core) * half_width + c * tile, tile), tile)
        to_in, to_out = weight_tiles(cols)
        peer_in[at, :] = to_in
        peer_out[:, at] = to_out

    swaps = [
        remote(peer_in, far_in, g_send.at[0], g_recv.at[0], {"dp": 1 - core}),
        remote(peer_out, far_out, g_send.at[1], g_recv.at[1], {"dp": 1 - core}),
    ]
    for copy in swaps:
        copy.start()

    for c in range(quarters):
        for d in range(1, INNER):
            back_copy(back_far, d, c).wait_recv()
        for d in (3, 1, 2):
            if (d, c) not in early:
                back_copy(back_pair, d, c).start()
        totals = [combine(1, half, c) for half in range(2)]

        @pl.when(is_inner)
        def _():
            for k in range(2):
                send_part(totals[k] + landed(from_end_near + k, c), k, from_cross + k, near, c)

        @pl.when(jnp.logical_not(is_inner))
        def _():
            for k in range(2):
                send_part(totals[k], k, from_end_near + k, partner, c)

    for c in range(quarters):
        for d in (3, 1, 2):
            back_copy(back_own, d, c).start()

    for copy in swaps:
        copy.wait_recv()

    @pl.loop(0, half_width // tile)
    def _(c):
        at = pl.ds(pl.multiple_of(c * tile, tile), tile)
        cols = pl.ds(pl.multiple_of(core * half_width + c * tile, tile), tile)
        to_in, to_out = weight_tiles(cols)
        gin_ref[at, :] = (to_in + far_in[at, :]).astype(jnp.bfloat16)
        gout_ref[:, at] = (to_out + far_out[:, at]).astype(jnp.bfloat16)

    for copy in stores:
        copy.start()

    for c in range(quarters):
        for d in range(1, INNER):
            back_copy(back_pair, d, c).wait_recv()
        total = combine(0, 1, c)

        @pl.when(is_inner)
        def _():
            send_part(total + landed(from_cross_far, c), 2, from_partner, partner, c)

        @pl.when(jnp.logical_not(is_inner))
        def _():
            send_part(total, 2, from_partner, partner, c)

    for c in range(quarters):
        cols = pl.ds(c * wide, wide)
        for d in range(1, INNER):
            back_copy(back_own, d, c).wait_recv()
        kept[:, cols] = combine(0, 0, c) + landed(from_partner, c)

        @pl.when(is_inner)
        def _():
            kept[:, cols] += landed(from_cross, c)

        tg_ref[:, cols] = kept[:, cols].astype(jnp.bfloat16)

    for s in others:
        meta_copy(s).wait_send()
    for slot in range(3):
        for c in range(quarters):
            part_copy(slot, from_partner, partner, c).wait_send()
    for a in range(2):
        own_copy(a, 0, partner).wait_send()

        @pl.when(is_inner)
        def _():
            own_copy(a, 1, cross).wait_send()
            pass_on(a, 2, partner, cross).wait_send()
            pass_on(a, 3, near, partner).wait_send()
            pass_on(a, 4, far, partner).wait_send()

    for d in range(1, INNER):
        for a in range(2):
            for piece in range(len(pieces)):
                plane_copy(a, piece, d).wait_send()
        for piece in range(3):
            for c in range(quarters):
                back_copy(piece, d, c).wait_send()
    for copy in swaps:
        copy.wait_send()
    for copy in stores:
        copy.wait()


def settle_kernel(*refs):
    half = len(refs) // 2
    for src, dst in zip(refs[:half], refs[half:]):
        dst[...] = src[...]


def settle(*arrays):
    parts = 4
    specs = [pl.BlockSpec((a.shape[0] // parts, a.shape[1]), lambda i: (i, 0)) for a in arrays]
    return pl.pallas_call(
        settle_kernel,
        grid=(parts,),
        out_shape=[jax.ShapeDtypeStruct(a.shape, a.dtype) for a in arrays],
        in_specs=specs,
        out_specs=specs,
    )(*arrays)


def fused(capacity, tokens, out_grad, expert_ids, gate_weights, w_in, w_out):
    hosts = PLANES * INNER
    count, width = tokens.shape
    ff = w_out.shape[1]
    hit = expert_ids.T[:, None, :] == jnp.arange(hosts, dtype=jnp.int32)[None, :, None]
    member = jnp.any(hit, axis=0)
    weight = jnp.sum(jnp.where(hit, gate_weights.T[:, None, :], 0.0), axis=0)
    order = jnp.arange(count, dtype=jnp.int32)
    earlier = (order[:, None] < order[None, :]).astype(jnp.bfloat16)
    rank = jnp.dot(member.astype(jnp.bfloat16), earlier, preferred_element_type=jnp.float32)
    code = jnp.where(member, rank, -1024.0)
    meta = jnp.concatenate([code, weight], axis=0)
    slots = 2 * INNER * 2 * capacity
    vmem = pl.BlockSpec(memory_space=pltpu.VMEM)
    hbm = pl.BlockSpec(memory_space=pl.ANY)
    quarters = width // 512
    bf16, f32, dma = jnp.bfloat16, jnp.float32, pltpu.SemaphoreType.DMA
    token_grad, grad_in, grad_out = pl.pallas_call(
        functools.partial(fused_kernel, capacity),
        out_shape=[
            jax.ShapeDtypeStruct((count, width), bf16),
            jax.ShapeDtypeStruct((width // 2, 2 * ff), bf16),
            jax.ShapeDtypeStruct((ff, width // 2), bf16),
        ],
        in_specs=[vmem] * 3 + [hbm] * 2,
        out_specs=[vmem, hbm, hbm],
        scratch_shapes=[
            pltpu.VMEM((width, 2 * ff), bf16),
            pltpu.VMEM((ff, width), bf16),
            pltpu.VMEM((width // 2, 2 * ff), bf16),
            pltpu.VMEM((ff, width // 2), bf16),
            pltpu.VMEM((slots // 2, 2 * ff), f32),
            pltpu.VMEM((PLANES, count, width), bf16),
            pltpu.VMEM((PLANES, count, width), bf16),
            pltpu.VMEM((PLANES, 2 * hosts, count), f32),
            pltpu.VMEM((slots, width), bf16),
            pltpu.VMEM((slots, width), bf16),
            pltpu.VMEM((slots, width), bf16),
            pltpu.VMEM((slots, width), bf16),
            pltpu.VMEM((slots, width), bf16),
            pltpu.VMEM((slots, width), bf16),
            pltpu.VMEM((slots, ff), bf16),
            pltpu.VMEM((slots, 2 * ff), bf16),
            pltpu.VMEM((3, count, width), bf16),
            pltpu.VMEM((5, count, width), bf16),
            pltpu.VMEM((count, width), f32),
            pltpu.VMEM((width // 2, 2 * ff), f32),
            pltpu.VMEM((ff, width // 2), f32),
            pltpu.VMEM((width // 2, 2 * ff), f32),
            pltpu.VMEM((ff, width // 2), f32),
            dma((2, 5)),
            dma((2, PLANES)),
            dma((PLANES,)),
            dma((PLANES,)),
            dma((2, 4, INNER)),
            dma((2, 4, INNER)),
            dma((3, INNER, quarters)),
            dma((3, INNER, quarters)),
            dma((3, quarters)),
            dma((5, quarters)),
            dma((2,)),
            dma((2,)),
            dma((4,)),
        ],
        compiler_params=pltpu.CompilerParams(
            collective_id=0, has_side_effects=True, vmem_limit_bytes=60 * 2**20
        ),
        cost_estimate=pl.CostEstimate(
            flops=2 * slots * width * ff * 8, bytes_accessed=12 * 2**20, transcendentals=slots * ff
        ),
    )(tokens, out_grad, meta, w_in[0], w_out[0])
    token_grad, grad_in, grad_out = settle(token_grad, grad_in, grad_out)
    return token_grad, grad_in[None], grad_out[None]


def body(tokens, out_grad, expert_ids, gate_weights, w_in, w_out):
    hosts = lax.axis_size("expert")
    token_count, model_width = tokens.shape
    capacity = 7 * token_count * expert_ids.shape[1] // (4 * hosts)
    if hosts == 16 and 2 * capacity % 16 == 0:
        return fused(capacity, tokens, out_grad, expert_ids, gate_weights, w_in, w_out)
    pick, slot_weight = selection(
        expert_ids, gate_weights, jnp.arange(hosts, dtype=jnp.int32), capacity
    )
    pick = pick.reshape(hosts * capacity, token_count)
    send_in = jnp.dot(pick, tokens, preferred_element_type=jnp.float32).astype(jnp.bfloat16)
    send_grad = (
        slot_weight.reshape(-1, 1) * jnp.dot(pick, out_grad, preferred_element_type=jnp.float32)
    ).astype(jnp.bfloat16)
    got_in = lax.all_to_all(send_in, "expert", split_axis=0, concat_axis=0, tiled=True)
    got_grad = lax.all_to_all(send_grad, "expert", split_axis=0, concat_axis=0, tiled=True)
    d_rows, grad_in, grad_out = backward_rows(got_in, got_grad, w_in[0], w_out[0])
    returned = lax.all_to_all(d_rows, "expert", split_axis=0, concat_axis=0, tiled=True)
    sum_in = lax.psum_scatter(grad_in, "dp", scatter_dimension=0, tiled=True)
    sum_out = lax.psum_scatter(grad_out, "dp", scatter_dimension=1, tiled=True)
    token_grad = lax.dot_general(
        pick, returned, (((0,), (0,)), ((), ())), preferred_element_type=jnp.float32
    ).astype(jnp.bfloat16)
    return (token_grad, sum_in.astype(jnp.bfloat16)[None], sum_out.astype(jnp.bfloat16)[None])


def solution(mesh):
    in_specs = (
        P(("dp", "expert"), None),
        P(("dp", "expert"), None),
        P(("dp", "expert"), None),
        P(("dp", "expert"), None),
        P("expert", None, None),
        P("expert", None, None),
    )
    out_specs = (P(("dp", "expert"), None), P("expert", "dp", None), P("expert", None, "dp"))
    return jax.shard_map(body, mesh=mesh, in_specs=in_specs, out_specs=out_specs, check_vma=False)
```

```python
import functools
import jax
import jax.numpy as jnp
from jax import lax
from jax.experimental import pallas as pl
from jax.experimental.pallas import tpu as pltpu
from jax.sharding import PartitionSpec as P


def silu_parts(gate_part):
    sigma = 1.0 / (1.0 + jnp.exp(-gate_part))
    return (gate_part * sigma, sigma * (1.0 + gate_part * (1.0 - sigma)))


def backward_rows(rows_in, rows_grad, weight_in, weight_out):
    hidden_width = weight_out.shape[0]
    joined = jnp.dot(rows_in, weight_in, preferred_element_type=jnp.float32)
    gate_part = joined[:, :hidden_width]
    up_part = joined[:, hidden_width:]
    activated, derivative = silu_parts(gate_part)
    hidden = (activated * up_part).astype(jnp.bfloat16)
    d_hidden = lax.dot_general(
        rows_grad, weight_out, (((1,), (1,)), ((), ())), preferred_element_type=jnp.float32
    )
    d_joined = jnp.concatenate(
        [d_hidden * up_part * derivative, d_hidden * activated], axis=1
    ).astype(jnp.bfloat16)
    d_rows = lax.dot_general(
        d_joined, weight_in, (((1,), (1,)), ((), ())), preferred_element_type=jnp.float32
    ).astype(jnp.bfloat16)
    grad_in = lax.dot_general(
        rows_in, d_joined, (((0,), (0,)), ((), ())), preferred_element_type=jnp.float32
    )
    grad_out = lax.dot_general(
        hidden, rows_grad, (((0,), (0,)), ((), ())), preferred_element_type=jnp.float32
    )
    return (d_rows, grad_in, grad_out)


def selection(ids, weights, experts, capacity):
    count = ids.shape[0]
    hit = ids[:, :, None] == experts[None, None, :]
    member = jnp.any(hit, axis=1)
    weight = jnp.sum(jnp.where(hit, weights[:, :, None], 0.0), axis=1)
    earlier = (
        jnp.arange(count, dtype=jnp.int32)[:, None] > jnp.arange(count, dtype=jnp.int32)[None, :]
    ).astype(jnp.bfloat16)
    rank = jnp.dot(earlier, member.astype(jnp.bfloat16), preferred_element_type=jnp.float32)
    rank = jnp.where(member, rank.astype(jnp.int32), -1)
    chosen = rank.T[:, None, :] == jnp.arange(capacity, dtype=jnp.int32)[None, :, None]
    slot_weight = jnp.sum(jnp.where(chosen, weight.T[:, None, :], 0.0), axis=2)
    return chosen.astype(jnp.bfloat16), slot_weight


PLANES = 4
INNER = 4
MESH = pl.DeviceIdType.MESH


def flipped(p, d):
    x, y = p % 2, p // 2
    if d % 2:
        x = 1 - x
    if d // 2:
        y = 1 - y
    return 2 * y + x


def fused_kernel(
    capacity,
    tok_ref,
    og_ref,
    meta_ref,
    w_in_hbm,
    w_out_hbm,
    tg_ref,
    gin_hbm,
    gout_hbm,
    w_in_ref,
    w_out_ref,
    gin_ref,
    gout_ref,
    joined_ref,
    ztok,
    zog,
    zmeta,
    send_in,
    send_gr,
    got_in,
    got_gr,
    d_rows,
    ret,
    hid,
    dj,
    part,
    part_got,
    kept,
    peer_in,
    peer_out,
    far_in,
    far_out,
    z_send,
    z_recv,
    meta_send,
    meta_recv,
    p_send,
    p_recv,
    r_send,
    r_recv,
    t_send,
    t_recv,
    g_send,
    g_recv,
    local_sem,
):
    me = lax.axis_index("expert")
    core = lax.axis_index("dp")
    z, p = me // INNER, me % INNER
    count, width = tok_ref.shape
    ff = w_out_ref.shape[0]
    rows = 2 * capacity
    block_rows = INNER * rows
    wide = 512
    odd = z % 2
    pair = z // 2
    partner = z + 1 - 2 * odd
    is_inner = jnp.logical_or(z == 1, z == 2)
    near = 2 - pair
    far = 3 * (1 - pair)
    zdev = lambda s: {"expert": s * INNER + p}
    pdev = lambda d: {"expert": z * INNER + flipped(p, d)}

    def remote(src, dst, send_sem, recv_sem, device):
        return pltpu.make_async_remote_copy(
            src_ref=src,
            dst_ref=dst,
            send_sem=send_sem,
            recv_sem=recv_sem,
            device_id=device,
            device_id_type=MESH,
        )

    loads = [
        pltpu.make_async_copy(w_in_hbm, w_in_ref, local_sem.at[0]),
        pltpu.make_async_copy(w_out_hbm, w_out_ref, local_sem.at[1]),
    ]
    stores = [
        pltpu.make_async_copy(gin_ref, gin_hbm, local_sem.at[2]),
        pltpu.make_async_copy(gout_ref, gout_hbm, local_sem.at[3]),
    ]
    barrier = pltpu.get_barrier_semaphore()
    for k in range(1, PLANES):
        pl.semaphore_signal(barrier, inc=1, device_id=zdev((z + k) % PLANES), device_id_type=MESH)
    for d in range(1, INNER):
        pl.semaphore_signal(barrier, inc=1, device_id=pdev(d), device_id_type=MESH)
    pl.semaphore_signal(barrier, inc=1, device_id={"dp": 1 - core}, device_id_type=MESH)
    pl.semaphore_wait(barrier, PLANES + INNER - 1)

    held = (ztok, zog)
    own = (tok_ref, og_ref)

    def meta_copy(s):
        return remote(meta_ref, zmeta.at[z], meta_send.at[s], meta_recv.at[z], zdev(s))

    def arrive_meta(s):
        remote(meta_ref, zmeta.at[s], meta_send.at[s], meta_recv.at[s], zdev(s)).wait_recv()

    def own_copy(a, k, to):
        return remote(own[a], held[a].at[z], z_send.at[a, k], z_recv.at[a, z], zdev(to))

    def pass_on(a, k, s, to):
        return remote(held[a].at[s], held[a].at[s], z_send.at[a, k], z_recv.at[a, s], zdev(to))

    def arrive(a, s):
        remote(held[a].at[s], held[a].at[s], z_send.at[a, 0], z_recv.at[a, s], zdev(s)).wait_recv()

    others = [(z + k) % PLANES for k in range(1, PLANES)]
    cross = near
    for s in others:
        meta_copy(s).start()
    for a in range(2):
        own_copy(a, 0, partner).start()

        @pl.when(is_inner)
        def _():
            own_copy(a, 1, cross).start()

    for copy in loads:
        copy.start()
    ztok[z] = tok_ref[...]
    zmeta[z] = meta_ref[...]

    row_id = lax.broadcasted_iota(jnp.int32, (rows, count), 0).astype(jnp.float32)

    def planes_of(b):
        return (z, partner) if b == 0 else (near, far)

    def chosen(s, half, d):
        expert = z * INNER + flipped(p, d)
        code = zmeta[s, pl.ds(expert, 1), :]
        return row_id == code + float(half * capacity)

    ready = capacity // 16 * 16
    pieces = tuple((b, *cut) for b in range(2) for cut in ((0, ready), (ready, rows - ready)))

    def plane_copy(a, piece, d):
        b, start, size = pieces[piece]
        src = (send_in, send_gr)[a]
        dst = (got_in, got_gr)[a]
        at = pl.ds(b * block_rows + d * rows + start, size)
        return remote(
            src.at[at], dst.at[at], p_send.at[a, piece, d], p_recv.at[a, piece, d], pdev(d)
        )

    def dispatch(a, piece):
        b, start, size = pieces[piece]
        planes = planes_of(b)[: 1 if start == 0 else 2]
        for d in (3, 1, 2, 0):
            picks = [chosen(s, half, d)[start : start + size] for half, s in enumerate(planes)]
            sels = [pick.astype(jnp.bfloat16) for pick in picks]
            if a == 1:
                expert = z * INNER + flipped(p, d) + PLANES * INNER
                scale = jnp.sum(
                    sum(
                        jnp.where(pick, zmeta[s, pl.ds(expert, 1), :], 0.0)
                        for pick, s in zip(picks, planes)
                    ),
                    axis=1,
                    keepdims=True,
                )
            out = ((got_in, got_gr) if d == 0 else (send_in, send_gr))[a]
            at = pl.ds(b * block_rows + d * rows + start, size)

            @pl.loop(0, width // wide)
            def _(c):
                cols = pl.ds(pl.multiple_of(c * wide, wide), wide)
                picked = sum(
                    jnp.dot(sel, held[a][s, :, cols], preferred_element_type=jnp.float32)
                    for sel, s in zip(sels, planes)
                )
                if a == 1:
                    picked = picked * scale
                out[at, cols] = picked.astype(jnp.bfloat16)

            if d:
                plane_copy(a, piece, d).start()

    dispatch(0, 0)
    zog[z] = og_ref[...]
    dispatch(1, 0)

    arrive(0, partner)

    @pl.when(is_inner)
    def _():
        pass_on(0, 2, partner, cross).start()

    arrive_meta(partner)
    dispatch(0, 1)
    arrive(1, partner)

    @pl.when(is_inner)
    def _():
        pass_on(1, 2, partner, cross).start()
        for a in range(2):
            arrive(a, near)
            pass_on(a, 3, near, partner).start()

    dispatch(1, 1)

    arrive_meta(near)
    arrive_meta(far)
    for a in range(2):

        @pl.when(jnp.logical_not(is_inner))
        def _():
            arrive(a, near)

        dispatch(a, 2)

        if a == 0:

            @pl.when(is_inner)
            def _():
                for other in range(2):
                    arrive(other, far)
                    pass_on(other, 4, far, partner).start()

    def arrive_rows(a, b):
        for d in range(1, INNER):
            for piece in range(len(pieces)):
                if pieces[piece][0] == b:
                    plane_copy(a, piece, d).wait_recv()

    tile_rows = block_rows // 2
    quarters = width // wide

    def joined_rows(b):
        @pl.loop(0, 2)
        def _(t):
            at = pl.ds(pl.multiple_of(b * block_rows + t * tile_rows, 16), tile_rows)
            joined_ref[pl.ds(pl.multiple_of(t * tile_rows, 16), tile_rows), :] = jnp.dot(
                got_in[at, :], w_in_ref[...], preferred_element_type=jnp.float32
            )

    def hidden_rows(b):
        @pl.loop(0, 2)
        def _(t):
            at = pl.ds(pl.multiple_of(b * block_rows + t * tile_rows, 16), tile_rows)
            here = pl.ds(pl.multiple_of(t * tile_rows, 16), tile_rows)
            gate_part, up_part = joined_ref[here, :ff], joined_ref[here, ff:]
            activated, derivative = silu_parts(gate_part)
            hid[at, :] = (activated * up_part).astype(jnp.bfloat16)
            d_hidden = lax.dot_general(
                got_gr[at, :],
                w_out_ref[...],
                (((1,), (1,)), ((), ())),
                preferred_element_type=jnp.float32,
            )
            dj[at, :ff] = (d_hidden * up_part * derivative).astype(jnp.bfloat16)
            dj[at, ff:] = (d_hidden * activated).astype(jnp.bfloat16)

    def input_rows(b, c):
        at = pl.ds(b * block_rows, block_rows)
        cols = pl.ds(c * wide, wide)
        d_rows[at, cols] = lax.dot_general(
            dj[at, :],
            w_in_ref[cols, :],
            (((1,), (1,)), ((), ())),
            preferred_element_type=jnp.float32,
        ).astype(jnp.bfloat16)

    back_own, back_pair, back_far = range(3)

    def back_copy(piece, d, c):
        b, start, size = ((0, 0, ready), (0, ready, rows - ready), (1, 0, rows))[piece]
        at = (pl.ds(b * block_rows + d * rows + start, size), pl.ds(c * wide, wide))
        return remote(
            d_rows.at[at], ret.at[at], r_send.at[piece, d, c], r_recv.at[piece, d, c], pdev(d)
        )

    from_end_near, from_end_far, from_partner, from_cross, from_cross_far = range(5)

    def part_copy(slot, land, to, c):
        cols = pl.ds(c * wide, wide)
        return remote(
            part.at[slot, :, cols],
            part_got.at[land, :, cols],
            t_send.at[slot, c],
            t_recv.at[land, c],
            zdev(to),
        )

    def landed(land, c):
        cols = pl.ds(c * wide, wide)
        part_copy(0, land, partner, c).wait_recv()
        return part_got[land, :, cols].astype(jnp.float32)

    def send_part(total, slot, land, to, c):
        part[slot, :, pl.ds(c * wide, wide)] = total.astype(jnp.bfloat16)
        part_copy(slot, land, to, c).start()

    def combine(b, half, c):
        s = planes_of(b)[half]
        cols = pl.ds(c * wide, wide)
        total = jnp.zeros((count, wide), jnp.float32)
        for d in range(INNER):
            start = ready if (b, half) == (0, 1) else 0
            at = pl.ds(b * block_rows + d * rows + start, rows - start)
            total = total + lax.dot_general(
                chosen(s, half, d)[start:].astype(jnp.bfloat16),
                (ret if d else d_rows)[at, cols],
                (((0,), (0,)), ((), ())),
                preferred_element_type=jnp.float32,
            )
        return total

    for copy in loads:
        copy.wait()
    arrive_rows(0, 0)
    joined_rows(0)
    arrive_rows(1, 0)
    hidden_rows(0)
    for c in range(quarters):
        input_rows(0, c)

    for a in range(2):

        @pl.when(jnp.logical_not(is_inner))
        def _():
            arrive(a, far)

        dispatch(a, 3)

    early = ((3, 0), (3, 1))
    arrive_rows(0, 1)
    joined_rows(1)
    arrive_rows(1, 1)
    for d, c in early:
        back_copy(back_pair, d, c).start()
    hidden_rows(1)
    for c in range(quarters):
        input_rows(1, c)
        for d in (3, 1, 2):
            back_copy(back_far, d, c).start()

    half_width = width // 2
    tile = 256

    def weight_tiles(cols):
        to_in = lax.dot_general(
            got_in[:, cols], dj[...], (((0,), (0,)), ((), ())), preferred_element_type=jnp.float32
        )
        to_out = lax.dot_general(
            hid[...], got_gr[:, cols], (((0,), (0,)), ((), ())), preferred_element_type=jnp.float32
        )
        return to_in, to_out

    @pl.loop(0, half_width // tile)
    def _(c):
        at = pl.ds(pl.multiple_of(c * tile, tile), tile)
        cols = pl.ds(pl.multiple_of((1 - core) * half_width + c * tile, tile), tile)
        to_in, to_out = weight_tiles(cols)
        peer_in[at, :] = to_in
        peer_out[:, at] = to_out

    swaps = [
        remote(peer_in, far_in, g_send.at[0], g_recv.at[0], {"dp": 1 - core}),
        remote(peer_out, far_out, g_send.at[1], g_recv.at[1], {"dp": 1 - core}),
    ]
    for copy in swaps:
        copy.start()

    for c in range(quarters):
        for d in range(1, INNER):
            back_copy(back_far, d, c).wait_recv()
        for d in (3, 1, 2):
            if (d, c) not in early:
                back_copy(back_pair, d, c).start()
        totals = [combine(1, half, c) for half in range(2)]

        @pl.when(is_inner)
        def _():
            for k in range(2):
                send_part(totals[k] + landed(from_end_near + k, c), k, from_cross + k, near, c)

        @pl.when(jnp.logical_not(is_inner))
        def _():
            for k in range(2):
                send_part(totals[k], k, from_end_near + k, partner, c)

    for c in range(quarters):
        for d in (3, 1, 2):
            back_copy(back_own, d, c).start()

    for copy in swaps:
        copy.wait_recv()

    @pl.loop(0, half_width // tile)
    def _(c):
        at = pl.ds(pl.multiple_of(c * tile, tile), tile)
        cols = pl.ds(pl.multiple_of(core * half_width + c * tile, tile), tile)
        to_in, to_out = weight_tiles(cols)
        gin_ref[at, :] = (to_in + far_in[at, :]).astype(jnp.bfloat16)
        gout_ref[:, at] = (to_out + far_out[:, at]).astype(jnp.bfloat16)

    for copy in stores:
        copy.start()

    for c in range(quarters):
        for d in range(1, INNER):
            back_copy(back_pair, d, c).wait_recv()
        total = combine(0, 1, c)

        @pl.when(is_inner)
        def _():
            send_part(total + landed(from_cross_far, c), 2, from_partner, partner, c)

        @pl.when(jnp.logical_not(is_inner))
        def _():
            send_part(total, 2, from_partner, partner, c)

    for c in range(quarters):
        cols = pl.ds(c * wide, wide)
        for d in range(1, INNER):
            back_copy(back_own, d, c).wait_recv()
        kept[:, cols] = combine(0, 0, c) + landed(from_partner, c)

        @pl.when(is_inner)
        def _():
            kept[:, cols] += landed(from_cross, c)

        tg_ref[:, cols] = kept[:, cols].astype(jnp.bfloat16)

    for s in others:
        meta_copy(s).wait_send()
    for slot in range(3):
        for c in range(quarters):
            part_copy(slot, from_partner, partner, c).wait_send()
    for a in range(2):
        own_copy(a, 0, partner).wait_send()

        @pl.when(is_inner)
        def _():
            own_copy(a, 1, cross).wait_send()
            pass_on(a, 2, partner, cross).wait_send()
            pass_on(a, 3, near, partner).wait_send()
            pass_on(a, 4, far, partner).wait_send()

    for d in range(1, INNER):
        for a in range(2):
            for piece in range(len(pieces)):
                plane_copy(a, piece, d).wait_send()
        for piece in range(3):
            for c in range(quarters):
                back_copy(piece, d, c).wait_send()
    for copy in swaps:
        copy.wait_send()
    for copy in stores:
        copy.wait()


def settle_kernel(*refs):
    half = len(refs) // 2
    for src, dst in zip(refs[:half], refs[half:]):
        dst[...] = src[...]


def settle(*arrays):
    parts = 2
    specs = [pl.BlockSpec((a.shape[0] // parts, a.shape[1]), lambda i: (i, 0)) for a in arrays]
    return pl.pallas_call(
        settle_kernel,
        grid=(parts,),
        out_shape=[jax.ShapeDtypeStruct(a.shape, a.dtype) for a in arrays],
        in_specs=specs,
        out_specs=specs,
    )(*arrays)


def fused(capacity, tokens, out_grad, expert_ids, gate_weights, w_in, w_out):
    hosts = PLANES * INNER
    count, width = tokens.shape
    ff = w_out.shape[1]
    hit = expert_ids.T[:, None, :] == jnp.arange(hosts, dtype=jnp.int32)[None, :, None]
    member = jnp.any(hit, axis=0)
    weight = jnp.sum(jnp.where(hit, gate_weights.T[:, None, :], 0.0), axis=0)
    order = jnp.arange(count, dtype=jnp.int32)
    earlier = (order[:, None] < order[None, :]).astype(jnp.bfloat16)
    rank = jnp.dot(member.astype(jnp.bfloat16), earlier, preferred_element_type=jnp.float32)
    code = jnp.where(member, rank, -1024.0)
    meta = jnp.concatenate([code, weight], axis=0)
    slots = 2 * INNER * 2 * capacity
    vmem = pl.BlockSpec(memory_space=pltpu.VMEM)
    hbm = pl.BlockSpec(memory_space=pl.ANY)
    quarters = width // 512
    bf16, f32, dma = jnp.bfloat16, jnp.float32, pltpu.SemaphoreType.DMA
    token_grad, grad_in, grad_out = pl.pallas_call(
        functools.partial(fused_kernel, capacity),
        out_shape=[
            jax.ShapeDtypeStruct((count, width), bf16),
            jax.ShapeDtypeStruct((width // 2, 2 * ff), bf16),
            jax.ShapeDtypeStruct((ff, width // 2), bf16),
        ],
        in_specs=[vmem] * 3 + [hbm] * 2,
        out_specs=[vmem, hbm, hbm],
        scratch_shapes=[
            pltpu.VMEM((width, 2 * ff), bf16),
            pltpu.VMEM((ff, width), bf16),
            pltpu.VMEM((width // 2, 2 * ff), bf16),
            pltpu.VMEM((ff, width // 2), bf16),
            pltpu.VMEM((slots // 2, 2 * ff), f32),
            pltpu.VMEM((PLANES, count, width), bf16),
            pltpu.VMEM((PLANES, count, width), bf16),
            pltpu.VMEM((PLANES, 2 * hosts, count), f32),
            pltpu.VMEM((slots, width), bf16),
            pltpu.VMEM((slots, width), bf16),
            pltpu.VMEM((slots, width), bf16),
            pltpu.VMEM((slots, width), bf16),
            pltpu.VMEM((slots, width), bf16),
            pltpu.VMEM((slots, width), bf16),
            pltpu.VMEM((slots, ff), bf16),
            pltpu.VMEM((slots, 2 * ff), bf16),
            pltpu.VMEM((3, count, width), bf16),
            pltpu.VMEM((5, count, width), bf16),
            pltpu.VMEM((count, width), f32),
            pltpu.VMEM((width // 2, 2 * ff), f32),
            pltpu.VMEM((ff, width // 2), f32),
            pltpu.VMEM((width // 2, 2 * ff), f32),
            pltpu.VMEM((ff, width // 2), f32),
            dma((2, 5)),
            dma((2, PLANES)),
            dma((PLANES,)),
            dma((PLANES,)),
            dma((2, 4, INNER)),
            dma((2, 4, INNER)),
            dma((3, INNER, quarters)),
            dma((3, INNER, quarters)),
            dma((3, quarters)),
            dma((5, quarters)),
            dma((2,)),
            dma((2,)),
            dma((4,)),
        ],
        compiler_params=pltpu.CompilerParams(
            collective_id=0, has_side_effects=True, vmem_limit_bytes=60 * 2**20
        ),
        cost_estimate=pl.CostEstimate(
            flops=2 * slots * width * ff * 8, bytes_accessed=12 * 2**20, transcendentals=slots * ff
        ),
    )(tokens, out_grad, meta, w_in[0], w_out[0])
    token_grad, grad_in, grad_out = settle(token_grad, grad_in, grad_out)
    return token_grad, grad_in[None], grad_out[None]


def body(tokens, out_grad, expert_ids, gate_weights, w_in, w_out):
    hosts = lax.axis_size("expert")
    token_count, model_width = tokens.shape
    capacity = 7 * token_count * expert_ids.shape[1] // (4 * hosts)
    if hosts == 16 and 2 * capacity % 16 == 0:
        return fused(capacity, tokens, out_grad, expert_ids, gate_weights, w_in, w_out)
    pick, slot_weight = selection(
        expert_ids, gate_weights, jnp.arange(hosts, dtype=jnp.int32), capacity
    )
    pick = pick.reshape(hosts * capacity, token_count)
    send_in = jnp.dot(pick, tokens, preferred_element_type=jnp.float32).astype(jnp.bfloat16)
    send_grad = (
        slot_weight.reshape(-1, 1) * jnp.dot(pick, out_grad, preferred_element_type=jnp.float32)
    ).astype(jnp.bfloat16)
    got_in = lax.all_to_all(send_in, "expert", split_axis=0, concat_axis=0, tiled=True)
    got_grad = lax.all_to_all(send_grad, "expert", split_axis=0, concat_axis=0, tiled=True)
    d_rows, grad_in, grad_out = backward_rows(got_in, got_grad, w_in[0], w_out[0])
    returned = lax.all_to_all(d_rows, "expert", split_axis=0, concat_axis=0, tiled=True)
    sum_in = lax.psum_scatter(grad_in, "dp", scatter_dimension=0, tiled=True)
    sum_out = lax.psum_scatter(grad_out, "dp", scatter_dimension=1, tiled=True)
    token_grad = lax.dot_general(
        pick, returned, (((0,), (0,)), ((), ())), preferred_element_type=jnp.float32
    ).astype(jnp.bfloat16)
    return (token_grad, sum_in.astype(jnp.bfloat16)[None], sum_out.astype(jnp.bfloat16)[None])


def solution(mesh):
    in_specs = (
        P(("dp", "expert"), None),
        P(("dp", "expert"), None),
        P(("dp", "expert"), None),
        P(("dp", "expert"), None),
        P("expert", None, None),
        P("expert", None, None),
    )
    out_specs = (P(("dp", "expert"), None), P("expert", "dp", None), P("expert", None, "dp"))
    return jax.shard_map(body, mesh=mesh, in_specs=in_specs, out_specs=out_specs, check_vma=False)
```
